1024 devices in a mesh: lat: 64 (over z, y_hi), rad: 16 (over x, y_lo, core).
Axes of the slice: x: 4, y: 4 (y_hi: 2, y_lo: 2; y = y_hi * 2 + y_lo), z: 32, core: 2. Of those that a mesh axis runs over, the one named last changes fastest.
Arguments:
- rhs_force: float32 [16, 65536], P('rad', 'lat'), may hold values from -96 to 96
- viscosity: float32 [16, 65536], P('rad', 'lat'), may hold values from 0.1 to 10
- initial_guess: float32 [16, 65536], P('rad', 'lat'), may hold values from -3 to 3
- glue_tile: int32 [64, 4], replicated, may hold values from 0 to 63, as said below
- glue_side: int32 [64, 4], replicated, may hold values from 0 to 3
- glue_flip: int32 [64, 4], replicated, may hold values from 0 to 1
Outputs:
- velocity: float32 [16, 65536], P('rad', 'lat')
The draws below stay inside these ranges and needn't reach their ends.
Inputs may be any that keep to these rules, and one draw needn't show every extreme that they name: `glue_tile`: every side of every tile is glued to exactly one other side: if side s of tile a meets side t of tile b, then side t of tile b meets side s of tile a with the same glue_flip code.
All inputs are finite; a program needn't handle non-finite values.
Results may differ from the reference program's by a relative error of at most 0.0003.
Values sent between devices are 32-bit elements; how exact they have to be, the bound alone decides.
No kernel may reach another device: no remote copies, remote signals or barrier semaphores. Data moves between devices by JAX's collectives and lax.ppermute only.
A program may use at most 32 MiB of HBM per device.

```python
import math
import jax
import jax.numpy as jnp

C = 32
NEWTON = 2
CG_ITERS = 4
TILES = 64
NR = 16


def glue_pairs(key):
    side_count = 4 * TILES
    side_order = jax.random.permutation(jax.random.fold_in(key, 11), side_count).astype(jnp.int32)
    pair_flips = jax.random.randint(jax.random.fold_in(key, 12), (side_count // 2,), 0, 2).astype(jnp.int32)
    first_sides = side_order[0::2]
    second_sides = side_order[1::2]
    partner = jnp.zeros((side_count,), jnp.int32).at[first_sides].set(second_sides).at[second_sides].set(first_sides)
    flipped = jnp.zeros((side_count,), jnp.int32).at[first_sides].set(pair_flips).at[second_sides].set(pair_flips)
    return (partner.reshape(TILES, 4), flipped.reshape(TILES, 4))


def draw_glue_tile(key, part):
    partner, flipped = glue_pairs(key)
    return (partner // 4).astype(jnp.int32)


def draw_glue_side(key, part):
    partner, flipped = glue_pairs(key)
    return (partner % 4).astype(jnp.int32)


def draw_glue_flip(key, part):
    partner, flipped = glue_pairs(key)
    return flipped.astype(jnp.int32)


def block_levels(rng, extent, cuts, smallest, top_value):
    loudness, own = 1.0, jax.random.fold_in(rng, 6)
    for position, shards_of in cuts:
        draws = jnp.exp(jax.random.uniform(jax.random.fold_in(own, position), (shards_of,), jnp.float32, smallest / len(cuts), top_value / len(cuts)))
        loudness = loudness * jnp.repeat(draws, extent[position] // shards_of).reshape([-1 if axis == position else 1 for axis in range(len(extent))])
    return loudness


def bell_draw(key, extent, scale, limit, shards=(), kind=jnp.bfloat16):
    factor_of = block_levels(key, extent, shards, -0.22, 0.18) if shards else 1.0
    entries = jax.random.normal(key, extent, jnp.float32) * scale * factor_of
    return jnp.minimum(jnp.maximum(entries, -limit), limit).astype(kind)


def setup_inputs(seed: int = 0) -> dict:
    seeds = jax.random.split(jax.random.key(seed), 7)
    rhs_force = bell_draw(seeds[0], (NR, TILES * C * C), 16.0, 96.0, ((0, 16), (1, 64)), jnp.float32)
    viscosity = jnp.clip(jnp.exp(math.log(10.0) - 4.6051702 * jax.random.uniform(seeds[1], (NR, TILES * C * C), jnp.float32) ** block_levels(seeds[1], (NR, TILES * C * C), ((0, 16), (1, 64)), -0.2, 0.2)), 0.1, 10.0)
    initial_guess = bell_draw(seeds[2], (NR, TILES * C * C), 1.0, 3.0, ((0, 16), (1, 64)), jnp.float32)
    glue_tile = draw_glue_tile(jax.random.fold_in(seeds[6], 71), 0)
    glue_side = draw_glue_side(jax.random.fold_in(seeds[6], 71), 0)
    glue_flip = draw_glue_flip(jax.random.fold_in(seeds[6], 71), 0)
    return dict(rhs_force=rhs_force, viscosity=viscosity, initial_guess=initial_guess, glue_tile=glue_tile, glue_side=glue_side, glue_flip=glue_flip)


cubic_weight = 8.0
radial_weight = 4.0
relax_factor = 0.8


def tile_sides(values, width):
    cell_total = width * width
    return jnp.stack([values[..., :width], values[..., cell_total - width:], values[..., ::width], values[..., width - 1::width]], axis=-2)


def table_ghosts(sides_all, gluing):
    glue_tile, glue_side, glue_flip = gluing
    picked = sides_all[:, glue_tile, glue_side, :]
    return jnp.where(glue_flip[None, :, :, None] == 1, picked[..., ::-1], picked)


def lateral_beside(values, ghost_rows, width):
    column = jnp.arange(width * width) % width
    zero_col = jnp.zeros(values.shape[:-1] + (1,), values.dtype)
    up_row = jnp.concatenate([ghost_rows[0], values[..., :-width]], axis=-1)
    down_row = jnp.concatenate([values[..., width:], ghost_rows[1]], axis=-1)
    left_col = jnp.where(column == 0, jnp.repeat(ghost_rows[2], width, axis=-1), jnp.concatenate([zero_col, values[..., :-1]], axis=-1))
    right_col = jnp.where(column == width - 1, jnp.repeat(ghost_rows[3], width, axis=-1), jnp.concatenate([values[..., 1:], zero_col], axis=-1))
    return (up_row, down_row, left_col, right_col)


def neighbours(values, width, gluing):
    ghosts = table_ghosts(tile_sides(values, width), gluing)
    ghost_rows = (ghosts[..., 0, :], ghosts[..., 1, :], ghosts[..., 2, :], ghosts[..., 3, :])
    zero_layer = jnp.zeros_like(values[:1])
    layer_above = jnp.concatenate([values[1:], zero_layer], axis=0)
    layer_below = jnp.concatenate([zero_layer, values[:-1]], axis=0)
    return lateral_beside(values, ghost_rows, width) + (layer_above, layer_below)


def conductances(viscous, width, gluing):
    beside = neighbours(viscous, width, gluing)
    lateral = [0.5 * (viscous + other) for other in beside[:4]]
    radial = [radial_weight * 0.5 * (viscous + other) for other in beside[4:]]
    return lateral + radial


def apply_op(values, conds, diagonal, width, gluing):
    beside = neighbours(values, width, gluing)
    coupled = conds[0] * beside[0] + conds[1] * beside[1] + conds[2] * beside[2] + conds[3] * beside[3] + conds[4] * beside[4] + conds[5] * beside[5]
    return diagonal * values - coupled


def restrict(values, width):
    half = width // 2
    shaped = values.reshape(values.shape[:-1] + (half, 2, half, 2))
    return jnp.sum(shaped, axis=(-3, -1)).reshape(values.shape[:-1] + (half * half,))


def prolong(values, half):
    shaped = values.reshape(values.shape[:-1] + (half, 1, half, 1))
    spread = jnp.broadcast_to(shaped, values.shape[:-1] + (half, 2, half, 2))
    return spread.reshape(values.shape[:-1] + (4 * half * half,))


def reference(rhs_force, viscosity, initial_guess, glue_tile, glue_side, glue_flip):
    cell_shape = (NR, TILES, C * C)
    half = C // 2
    gluing = (glue_tile, glue_side, glue_flip)
    forcing = rhs_force.reshape(cell_shape)
    velocity = initial_guess.reshape(cell_shape)
    conds = conductances(viscosity.reshape(cell_shape), C, gluing)
    cond_total = conds[0] + conds[1] + conds[2] + conds[3] + conds[4] + conds[5]
    for newton_step in range(NEWTON):
        cubic_term = cubic_weight * velocity * velocity
        damping = 3.0 * cubic_term
        residual = forcing - apply_op(velocity, conds, cond_total + cubic_term, C, gluing)
        diag_j = cond_total + damping
        smoothed = relax_factor * residual / diag_j
        remain = residual - apply_op(smoothed, conds, diag_j, C, gluing)
        coarse_rhs = restrict(remain, C)

        def coarse_op(values, diag_j=diag_j):
            return restrict(apply_op(prolong(values, half), conds, diag_j, C, gluing), C)

        solution = jnp.zeros_like(coarse_rhs)
        residual_c = coarse_rhs
        direction = coarse_rhs
        norm_now = jnp.sum(residual_c * residual_c)
        for cg_step in range(CG_ITERS):
            image_dir = coarse_op(direction)
            step_size = norm_now / jnp.sum(direction * image_dir)
            solution = solution + step_size * direction
            residual_c = residual_c - step_size * image_dir
            if cg_step + 1 < CG_ITERS:
                norm_next = jnp.sum(residual_c * residual_c)
                direction = residual_c + (norm_next / norm_now) * direction
                norm_now = norm_next
        velocity = velocity + smoothed + prolong(solution, half)
    return velocity.reshape(NR, TILES * C * C)
```

```python
import functools

import jax
import jax.numpy as jnp
from jax import lax
from jax.experimental import pallas as pl
from jax.experimental.pallas import tpu as pltpu
from jax.sharding import PartitionSpec as P

C = 32
HALF = 16
TILES = 64
NR = 16
CELLS = C * C
COARSE = HALF * HALF
LANES = 128
CG_ITERS = 4

cubic_weight = 8.0
radial_weight = 4.0
relax_factor = 0.8


def low(x):
    return lax.broadcasted_iota(jnp.int32, x.shape, x.ndim - 1) < TILES


def swap(x):
    return pltpu.roll(x, TILES, x.ndim - 1)


def pack(a, b):
    return jnp.where(low(a), a, b)


def first_twin(x):
    return jnp.where(low(x), x, swap(x))


def second_twin(x):
    return jnp.where(low(x), swap(x), x)


def glued(values, gluing):
    rows = values.shape[0]
    high = values.astype(jnp.bfloat16)
    rest = values - high.astype(jnp.float32)
    middle = rest.astype(jnp.bfloat16)
    lowest = (rest - middle.astype(jnp.float32)).astype(jnp.bfloat16)
    moved = jnp.dot(
        jnp.concatenate([high, middle, lowest], axis=0), gluing, preferred_element_type=jnp.float32
    )
    return moved[:rows] + (moved[rows : 2 * rows] + moved[2 * rows :])


def fine_ghosts(pad_ref, west_ref, east_ref, gluing, flips):
    north, south = pad_ref[C : 2 * C], pad_ref[CELLS : CELLS + C]
    west, east = pad_ref[pl.ds(C, C, stride=C)], pad_ref[pl.ds(2 * C - 1, C, stride=C)]
    moved = glued(jnp.concatenate([pack(north, south), pack(west, east)], axis=1), gluing)
    mirror = lax.broadcasted_iota(jnp.int32, (C, C), 0) + lax.broadcasted_iota(jnp.int32, (C, C), 1) == C - 1
    mirrored = jnp.dot(
        mirror.astype(jnp.float32), moved, precision=lax.Precision.HIGHEST, preferred_element_type=jnp.float32
    )
    pairs = []
    for pair in range(2):
        lanes = slice(pair * LANES, (pair + 1) * LANES)
        flip = pack(flips[2 * pair : 2 * pair + 1], flips[2 * pair + 1 : 2 * pair + 2])
        pairs.append(jnp.where(flip > 0, mirrored[:, lanes], moved[:, lanes]))
    pad_ref[0:C] = first_twin(pairs[0])
    pad_ref[CELLS + C : CELLS + 2 * C] = second_twin(pairs[0])
    west_ref[...] = first_twin(pairs[1])
    east_ref[...] = second_twin(pairs[1])


def row_of(i):
    return pl.ds(pl.multiple_of(i * C, C), C)


def lateral(pad_ref, west_ref, east_ref, i):
    own = pad_ref[row_of(i + 1)]
    column = lax.broadcasted_iota(jnp.int32, own.shape, 0)
    west = jnp.where(column == 0, west_ref[pl.ds(i, 1)], pltpu.roll(own, 1, 0))
    east = jnp.where(column == C - 1, east_ref[pl.ds(i, 1)], pltpu.roll(own, C - 1, 0))
    return own, (pad_ref[row_of(i)], pad_ref[row_of(i + 2)], west, east)


def coupled(conds, beside):
    total = conds[0] * beside[0]
    for cond, value in zip(conds[1:], beside[1:]):
        total = total + cond * value
    return total


def smooth_row(i, force, conds, cond_total, own, beside, residual_ref, smoothed_ref):
    cubic = cubic_weight * own * own
    residual = force - ((cond_total + cubic) * own - coupled(conds, beside))
    residual_ref[row_of(i)] = residual
    smoothed_ref[row_of(i)] = relax_factor * residual / (cond_total + 3.0 * cubic)


def pack_halves(smoothed_ref, packed_ref):
    packed_ref[...] = pack(smoothed_ref[: CELLS // 2], smoothed_ref[CELLS // 2 :])


def unpack_row(packed_ref, i, upper):
    block = packed_ref[row_of(i)]
    return second_twin(block) if upper else first_twin(block)


def unpack_halves(packed_ref, target_ref):
    target_ref[: CELLS // 2] = first_twin(packed_ref[...])
    target_ref[CELLS // 2 :] = second_twin(packed_ref[...])


def every(ref, start, count):
    return ref[pl.ds(start, count, stride=2)]


def spread_kernel(arrived_ref, pair_ref, force_ref):
    for group in range(8):
        parts = [arrived_ref[pl.ds(8 * field + group, TILES, stride=24)] for field in range(3)]
        cells = slice(group * LANES, (group + 1) * LANES)
        pair_ref[cells] = jnp.concatenate(parts[:2], axis=0).T
        force_ref[cells] = jnp.concatenate([parts[2], parts[2]], axis=0).T


def first_kernel(
    pair_ref, force_ref, above_ref, below_ref, gluing_ref, flips_ref,
    conds_ref, total_ref, residual_ref, smoothed_ref, packed_ref, faces_ref, face_total_ref,
    viscous, viscous_west, viscous_east, velocity, west, east,
):
    gluing, flips = gluing_ref[...], flips_ref[...]
    viscous[C : C + CELLS] = first_twin(pair_ref[...])
    velocity[C : C + CELLS] = second_twin(pair_ref[...])
    fine_ghosts(viscous, viscous_west, viscous_east, gluing, flips)
    fine_ghosts(velocity, west, east, gluing, flips)

    @pl.loop(0, C)
    def _(i):
        above, below = above_ref[row_of(i)], below_ref[row_of(i)]
        own, beside = lateral(viscous, viscous_west, viscous_east, i)
        conds = [0.5 * (own + other) for other in beside]
        conds += [radial_weight * 0.5 * (own + other) for other in (first_twin(above), first_twin(below))]
        cond_total = conds[0]
        for cond in conds[1:]:
            cond_total = cond_total + cond
        for direction in range(6):
            conds_ref[direction, row_of(i)] = conds[direction]
        total_ref[row_of(i)] = cond_total
        own, beside = lateral(velocity, west, east, i)
        beside = beside + (second_twin(above), second_twin(below))
        smooth_row(i, force_ref[row_of(i)], conds, cond_total, own, beside, residual_ref, smoothed_ref)

    pack_halves(smoothed_ref, packed_ref)
    ups = []
    for big in range(HALF):
        upper, lower = big * 2 * C, big * 2 * C + C
        cells = slice(big * HALF, (big + 1) * HALF)

        def both(direction, start):
            return every(conds_ref.at[direction], start, HALF) + every(conds_ref.at[direction], start + 1, HALF)

        def column(direction, start):
            return every(conds_ref.at[direction], upper + start, HALF) + every(
                conds_ref.at[direction], lower + start, HALF
            )

        north, south = both(0, upper), both(1, lower)
        west_face, east_face = column(2, 0), column(3, 1)
        up, down = both(4, upper) + both(4, lower), both(5, upper) + both(5, lower)
        faces_ref[cells] = pack(south, east_face)
        if big == 0:
            faces_ref[COARSE + COARSE // 2 : COARSE + COARSE // 2 + HALF] = north
        viscous_west[big : big + 1] = west_face[0:1]
        ups.append(up)
        face_total_ref[cells] = north + south + west_face + east_face + up + down
    for big in range(HALF // 2):
        start = COARSE + big * HALF
        faces_ref[start : start + HALF] = pack(ups[big], ups[big + HALF // 2])
    start = COARSE + COARSE // 2
    faces_ref[start : start + HALF] = pack(faces_ref[start : start + HALF], viscous_west[0:HALF])


def remain_kernel(
    conds_ref, total_ref, velocity_ref, residual_ref, smoothed_ref, above_ref, below_ref, face_total_ref,
    gluing_ref, flips_ref, coarse_ref, pad, west, east, above, below, remain, damping, *, paired,
):
    pad[C : C + CELLS] = smoothed_ref[...]
    unpack_halves(above_ref, above)
    unpack_halves(below_ref, below)
    fine_ghosts(pad, west, east, gluing_ref[...], flips_ref[...])

    @pl.loop(0, C)
    def _(i):
        velocity = velocity_ref[row_of(i)]
        if paired:
            velocity = second_twin(velocity)
        damp = 3.0 * (cubic_weight * velocity * velocity)
        own, beside = lateral(pad, west, east, i)
        beside = beside + (above[row_of(i)], below[row_of(i)])
        conds = [conds_ref[direction, row_of(i)] for direction in range(6)]
        image = (total_ref[row_of(i)] + damp) * own - coupled(conds, beside)
        remain[row_of(i)] = residual_ref[row_of(i)] - image
        damping[row_of(i)] = damp

    for big in range(HALF):
        sums = []
        for ref in (remain, damping):
            start = big * 2 * C
            sums.append(
                every(ref, start, HALF)
                + every(ref, start + 1, HALF)
                + every(ref, start + C, HALF)
                + every(ref, start + C + 1, HALF)
            )
        cells = slice(big * HALF, (big + 1) * HALF)
        coarse_ref[cells] = pack(sums[0], face_total_ref[cells] + sums[1])


def layered(ref, layer_pair, start, count):
    return ref[2 * layer_pair, start : start + count], ref[2 * layer_pair + 1, start : start + count]


def faces_kernel(gathered_ref, rows_ref, columns_ref, up_ref, down_ref):
    middle, last = COARSE, COARSE + COARSE // 2
    for sub in range(8):
        a, b = layered(gathered_ref, sub, 0, COARSE)
        rows_ref[pl.ds(LANES + sub, COARSE, stride=8)] = pack(a, swap(b))
        east = pack(swap(a), b)
        for big in range(HALF):
            columns_ref[big, pl.ds(8 + sub, HALF, stride=8)] = east[big * HALF : (big + 1) * HALF]
        a, b = layered(gathered_ref, sub, middle, COARSE // 2)
        up_ref[pl.ds(sub, COARSE // 2, stride=8)] = pack(a, swap(b))
        up_ref[pl.ds(8 * COARSE // 2 + sub, COARSE // 2, stride=8)] = pack(swap(a), b)
        a, b = layered(gathered_ref, sub, last, HALF)
        rows_ref[pl.ds(sub, HALF, stride=8)] = pack(a, swap(b))
        west = pack(swap(a), b)
        for big in range(HALF):
            columns_ref[big, sub : sub + 1] = west[big : big + 1]
    row = lax.broadcasted_iota(jnp.int32, (8, LANES), 0)
    lane = lax.broadcasted_iota(jnp.int32, (8, LANES), 1)
    outside = (row == 7) & (lane >= TILES)

    @pl.loop(0, COARSE)
    def _(cell):
        here = pl.ds(pl.multiple_of(cell * 8, 8), 8)
        up = jnp.where(outside, 0.0, up_ref[here])
        up_ref[here] = up
        swapped = swap(up)
        down_ref[here] = jnp.where(lane < TILES, pltpu.roll(swapped, 1, 0), swapped)


def coarse_ghosts(pad, gluing, flips):
    side = HALF * 8
    inner = slice(8, 8 + side)
    north, south = pad[1, inner], pad[HALF, inner]
    west = pad[1 : HALF + 1, 8:16].reshape(side, LANES)
    east = pad[1 : HALF + 1, side : side + 8].reshape(side, LANES)
    first = jnp.concatenate([pack(north, swap(south)), pack(west, swap(east))], axis=1)
    second = jnp.concatenate([pack(swap(north), south), pack(swap(west), east)], axis=1)
    moved = glued(jnp.concatenate([first, second], axis=0), gluing)
    ghosts = []
    for pair in range(2):
        lanes = slice(pair * LANES, (pair + 1) * LANES)
        a, b = moved[:side, lanes], moved[side:, lanes]
        ghosts += [pack(a, swap(b)), pack(swap(a), b)]
    for number, ghost in enumerate(ghosts):
        flip = jnp.broadcast_to(flips[number : number + 1], (8, LANES)) > 0
        for k in range(HALF):
            other = HALF - 1 - k
            value = jnp.where(flip, ghost[8 * other : 8 * other + 8], ghost[8 * k : 8 * k + 8])
            if number < 2:
                pad[0 if number == 0 else HALF + 1, 8 + 8 * k : 16 + 8 * k] = value
            else:
                column = 0 if number == 2 else 8 + side
                pad[1 + k, column : column + 8] = value


def total_of(x):
    return jnp.sum(jnp.sum(x, axis=0, keepdims=True), axis=1, keepdims=True)


def folded(x):
    return jnp.sum(x.reshape(x.shape[0] // 8, 8, LANES), axis=0)


def solve_coarse(
    gathered_ref, rows_ref, columns_ref, up_ref, down_ref, gluing, flips, pad, diagonal, image, residual, solution
):
    side = HALF * 8
    inner = slice(8, 8 + side)
    chunk = 64
    for sub in range(8):
        a, b = layered(gathered_ref, sub, 0, COARSE)
        residual[pl.ds(sub, COARSE, stride=8)] = pack(a, swap(b))
        diagonal[pl.ds(sub, COARSE, stride=8)] = pack(swap(a), b)

    zero = jnp.zeros((8, LANES), jnp.float32)

    def start(big, norm):
        here = pl.ds(pl.multiple_of(big * side, side), side)
        values = residual[here]
        pad[big + 1, inner] = values
        solution[here] = jnp.zeros_like(values)
        return norm + folded(values * values)

    norm = total_of(lax.fori_loop(0, HALF, start, zero))

    def apply_row(big, total):
        for part in range(side // chunk):
            first = part * chunk
            here = pl.ds(pl.multiple_of(big * side + first, chunk), chunk)
            own = pad[big + 1, 8 + first : 8 + first + chunk]
            swapped = swap(own).reshape(chunk // 8, 8, LANES)
            before = pltpu.roll(swapped, 1, 1).reshape(chunk, LANES)
            after = pltpu.roll(swapped, 7, 1).reshape(chunk, LANES)
            swapped = swapped.reshape(chunk, LANES)
            below = pl.ds(pl.multiple_of((big + 1) * side + first, chunk), chunk)
            value = (
                rows_ref[here] * pad[big, 8 + first : 8 + first + chunk]
                + rows_ref[below] * pad[big + 2, 8 + first : 8 + first + chunk]
                + columns_ref[big, first : first + chunk] * pad[big + 1, first : first + chunk]
                + columns_ref[big, 8 + first : 8 + first + chunk] * pad[big + 1, 16 + first : 16 + first + chunk]
                + up_ref[here] * pack(swapped, after)
                + down_ref[here] * pack(before, swapped)
            )
            value = diagonal[here] * own - value
            image[here] = value
            total = total + folded(own * value)
        return total

    for step in range(CG_ITERS):
        coarse_ghosts(pad, gluing, flips)
        length = norm / total_of(lax.fori_loop(0, HALF, apply_row, zero))

        def advance(big, total, length=length):
            here = pl.ds(pl.multiple_of(big * side, side), side)
            solution[here] = solution[here] + length * pad[big + 1, inner]
            values = residual[here] - length * image[here]
            residual[here] = values
            return total + folded(values * values)

        following = total_of(lax.fori_loop(0, HALF, advance, zero))
        if step + 1 < CG_ITERS:
            ratio = following / norm
            norm = following

            def turn(big, carry, ratio=ratio):
                here = pl.ds(pl.multiple_of(big * side, side), side)
                pad[big + 1, inner] = residual[here] + ratio * pad[big + 1, inner]
                return carry

            lax.fori_loop(0, HALF, turn, 0)


def prolong_layer(solution, layer, target):
    inside = (layer >= 0) & (layer < NR)
    place = jnp.clip(layer, 0, NR - 1)
    values = solution[pl.ds(place // 2, COARSE, stride=8)]
    values = jnp.where(place % 2 == 0, first_twin(values), second_twin(values))
    values = jnp.where(inside, values, 0.0)
    for big in range(HALF):
        row = values[big * HALF : (big + 1) * HALF]
        for start in (0, 1, C, C + 1):
            target[pl.ds(big * 2 * C + start, HALF, stride=2)] = row


COARSE_SCRATCH = [
    pltpu.VMEM((HALF + 2, (HALF + 2) * 8, LANES), jnp.float32),
    *[pltpu.VMEM((COARSE * 8, LANES), jnp.float32) for _ in range(4)],
]


def step_kernel(
    place_ref, gathered_ref, rows_ref, columns_ref, up_ref, down_ref, gluing_ref, flips_ref,
    pair_ref, above_ref, below_ref, smoothed_ref, smoothed_above_ref, smoothed_below_ref, force_ref, conds_ref,
    total_ref, new_velocity_ref, new_residual_ref, new_smoothed_ref, packed_ref,
    pad, diagonal, image, residual, solution, velocity, west, east, above, below, spread,
):
    gluing, flips = gluing_ref[...], flips_ref[...]
    solve_coarse(
        gathered_ref, rows_ref, columns_ref, up_ref, down_ref, gluing, flips, pad, diagonal, image, residual, solution
    )
    layer = place_ref[0]
    prolong_layer(solution, layer, spread)
    velocity[C : C + CELLS] = second_twin(pair_ref[...]) + smoothed_ref[...] + spread[...]
    new_velocity_ref[...] = velocity[C : C + CELLS]
    for shift, pairs, smooth, target in (
        (1, above_ref, smoothed_above_ref, above),
        (-1, below_ref, smoothed_below_ref, below),
    ):
        prolong_layer(solution, layer + shift, spread)
        unpack_halves(smooth, target)
        target[...] = second_twin(pairs[...]) + target[...] + spread[...]
    fine_ghosts(velocity, west, east, gluing, flips)

    @pl.loop(0, C)
    def _(i):
        own, beside = lateral(velocity, west, east, i)
        beside = beside + (above[row_of(i)], below[row_of(i)])
        conds = [conds_ref[direction, row_of(i)] for direction in range(6)]
        smooth_row(
            i, force_ref[row_of(i)], conds, total_ref[row_of(i)], own, beside, new_residual_ref, new_smoothed_ref
        )

    pack_halves(new_smoothed_ref, packed_ref)


def last_kernel(
    place_ref, gathered_ref, rows_ref, columns_ref, up_ref, down_ref, gluing_ref, flips_ref, velocity_ref,
    smoothed_ref, out_ref, pad, diagonal, image, residual, solution, spread, turned,
):
    solve_coarse(
        gathered_ref, rows_ref, columns_ref, up_ref, down_ref, gluing_ref[...], flips_ref[...],
        pad, diagonal, image, residual, solution,
    )
    prolong_layer(solution, place_ref[0], spread)
    for group in range(8):
        cells = slice(group * LANES, (group + 1) * LANES)
        turned[cells] = (velocity_ref[cells] + smoothed_ref[cells] + spread[cells]).T
    for group in range(8):
        out_ref[group : group + 1] = turned[pl.ds(group * LANES + place_ref[1], 1)]


def call(kernel, outs, scratch, args, scalars=0):
    vmem = pl.BlockSpec(memory_space=pltpu.VMEM)
    shapes = [jax.ShapeDtypeStruct(shape, jnp.float32) for shape in outs]
    return pl.pallas_call(
        kernel,
        out_shape=shapes,
        in_specs=[pl.BlockSpec(memory_space=pltpu.SMEM)] * scalars + [vmem] * (len(args) - scalars),
        out_specs=[vmem] * len(outs),
        scratch_shapes=scratch,
        compiler_params=pltpu.CompilerParams(vmem_limit_bytes=44 << 20),
    )(*args)


PADDED = (CELLS + 2 * C, LANES)
FINE = (CELLS, LANES)
PACKED = (CELLS // 2, LANES)
EDGE = (C, LANES)
FACES = (COARSE + COARSE // 2 + HALF, LANES)


def buffers(*shapes):
    return [pltpu.VMEM(shape, jnp.float32) for shape in shapes]


def spread_layer(arrived):
    return call(spread_kernel, [FINE, FINE], [], [arrived])


def first_stage(pair, force, above, below, gluing, flips):
    outs = [(6,) + FINE, FINE, FINE, FINE, PACKED, FACES, (COARSE, LANES)]
    scratch = buffers(PADDED, EDGE, EDGE, PADDED, EDGE, EDGE)
    return call(first_kernel, outs, scratch, [pair, force, above, below, gluing, flips])


def remain_stage(paired, *args):
    scratch = buffers(PADDED, EDGE, EDGE, FINE, FINE, FINE, FINE)
    return call(functools.partial(remain_kernel, paired=paired), [(COARSE, LANES)], scratch, list(args))[0]


def faces_stage(gathered):
    outs = [((HALF + 1) * HALF * 8, LANES), (HALF, (HALF + 1) * 8, LANES)] + [(COARSE * 8, LANES)] * 2
    return call(faces_kernel, outs, [], [gathered])


def step_stage(*args):
    scratch = COARSE_SCRATCH + buffers(PADDED, EDGE, EDGE, FINE, FINE, FINE)
    return call(step_kernel, [FINE, FINE, FINE, PACKED], scratch, list(args), 1)


def last_stage(*args):
    scratch = COARSE_SCRATCH + buffers(FINE, FINE)
    return call(last_kernel, [(8, LANES)], scratch, list(args), 1)[0]


def gluing_tables(glue_tile, glue_side, glue_flip):
    source = (glue_side * TILES + glue_tile).T.reshape(1, 4 * TILES)
    gluing = (jnp.arange(4 * TILES)[:, None] == source).astype(jnp.bfloat16)
    flips = glue_flip.T.astype(jnp.float32)
    flips = jnp.concatenate([flips, flips], axis=1)
    return gluing, jnp.concatenate([flips, flips], axis=0)


def gather(values, axis):
    count = lax.axis_size(axis)
    return lax.all_to_all(
        jnp.broadcast_to(values[None], (count,) + values.shape), axis, split_axis=0, concat_axis=0, tiled=True
    )


def radial(values):
    backward = [(layer + 1, layer) for layer in range(NR - 1)]
    forward = [(layer, layer + 1) for layer in range(NR - 1)]
    return lax.ppermute(values, "rad", backward), lax.ppermute(values, "rad", forward)


def on_device(rhs_force, viscosity, initial_guess, glue_tile, glue_side, glue_flip):
    gluing, flips = gluing_tables(glue_tile, glue_side, glue_flip)
    place = jnp.stack([lax.axis_index("rad"), lax.axis_index("lat")]).astype(jnp.int32)
    own = jnp.concatenate([field.reshape(8, LANES) for field in (viscosity, initial_guess, rhs_force)], axis=0)
    pair, force = spread_layer(gather(own, "lat").reshape(TILES * 24, LANES))
    above, below = radial(pair)
    conds, total, residual, smoothed, packed, faces, face_total = first_stage(
        pair, force, above, below, gluing, flips
    )
    smoothed_above, smoothed_below = radial(packed)
    coefficients = faces_stage(gather(faces, "rad"))
    coarse = remain_stage(
        True, conds, total, pair, residual, smoothed, smoothed_above, smoothed_below, face_total, gluing, flips
    )
    velocity, residual, smoothed, packed = step_stage(
        place, gather(coarse, "rad"), *coefficients, gluing, flips, pair, above, below, smoothed, smoothed_above,
        smoothed_below, force, conds, total,
    )
    smoothed_above, smoothed_below = radial(packed)
    coarse = remain_stage(
        False, conds, total, velocity, residual, smoothed, smoothed_above, smoothed_below, face_total, gluing, flips
    )
    out = last_stage(place, gather(coarse, "rad"), *coefficients, gluing, flips, velocity, smoothed)
    return out.reshape(1, CELLS)


def solution(mesh):
    return jax.shard_map(
        on_device,
        mesh=mesh,
        in_specs=(P("rad", "lat"), P("rad", "lat"), P("rad", "lat"), P(), P(), P()),
        out_specs=P("rad", "lat"),
        check_vma=False,
    )
```

```python
import functools

import jax
import jax.numpy as jnp
from jax import lax
from jax.experimental import pallas as pl
from jax.experimental.pallas import tpu as pltpu
from jax.sharding import PartitionSpec as P

C = 32
HALF = 16
TILES = 64
NR = 16
CHIPS = NR // 2
CELLS = C * C
COARSE = HALF * HALF
LANES = 128
CG_ITERS = 4

cubic_weight = 8.0
radial_weight = 4.0
relax_factor = 0.8


def low(x):
    return lax.broadcasted_iota(jnp.int32, x.shape, x.ndim - 1) < TILES


def swap(x):
    return pltpu.roll(x, TILES, x.ndim - 1)


def pack(a, b):
    return jnp.where(low(a), a, b)


def first_twin(x):
    return jnp.where(low(x), x, swap(x))


def second_twin(x):
    return jnp.where(low(x), swap(x), x)


def glued(values, gluing):
    rows = values.shape[0]
    high = values.astype(jnp.bfloat16)
    rest = values - high.astype(jnp.float32)
    middle = rest.astype(jnp.bfloat16)
    lowest = (rest - middle.astype(jnp.float32)).astype(jnp.bfloat16)
    moved = jnp.dot(
        jnp.concatenate([high, middle, lowest], axis=0), gluing, preferred_element_type=jnp.float32
    )
    return moved[:rows] + (moved[rows : 2 * rows] + moved[2 * rows :])


def fine_ghosts(pad_ref, west_ref, east_ref, gluing, flips):
    north, south = pad_ref[C : 2 * C], pad_ref[CELLS : CELLS + C]
    west, east = pad_ref[pl.ds(C, C, stride=C)], pad_ref[pl.ds(2 * C - 1, C, stride=C)]
    moved = glued(jnp.concatenate([pack(north, south), pack(west, east)], axis=1), gluing)
    mirror = lax.broadcasted_iota(jnp.int32, (C, C), 0) + lax.broadcasted_iota(jnp.int32, (C, C), 1) == C - 1
    mirrored = jnp.dot(
        mirror.astype(jnp.float32), moved, precision=lax.Precision.HIGHEST, preferred_element_type=jnp.float32
    )
    pairs = []
    for pair in range(2):
        lanes = slice(pair * LANES, (pair + 1) * LANES)
        flip = pack(flips[2 * pair : 2 * pair + 1], flips[2 * pair + 1 : 2 * pair + 2])
        pairs.append(jnp.where(flip > 0, mirrored[:, lanes], moved[:, lanes]))
    pad_ref[0:C] = first_twin(pairs[0])
    pad_ref[CELLS + C : CELLS + 2 * C] = second_twin(pairs[0])
    west_ref[...] = first_twin(pairs[1])
    east_ref[...] = second_twin(pairs[1])


def row_of(i):
    return pl.ds(pl.multiple_of(i * C, C), C)


def lateral(pad_ref, west_ref, east_ref, i):
    own = pad_ref[row_of(i + 1)]
    column = lax.broadcasted_iota(jnp.int32, own.shape, 0)
    west = jnp.where(column == 0, west_ref[pl.ds(i, 1)], pltpu.roll(own, 1, 0))
    east = jnp.where(column == C - 1, east_ref[pl.ds(i, 1)], pltpu.roll(own, C - 1, 0))
    return own, (pad_ref[row_of(i)], pad_ref[row_of(i + 2)], west, east)


def coupled(conds, beside):
    total = conds[0] * beside[0]
    for cond, value in zip(conds[1:], beside[1:]):
        total = total + cond * value
    return total


def smooth_row(i, force, cond_total, own, image, residual_ref, smoothed_ref):
    cubic = cubic_weight * own * own
    residual = force - ((cond_total + cubic) * own - image)
    residual_ref[row_of(i)] = residual
    smoothed_ref[row_of(i)] = relax_factor * residual / (cond_total + 3.0 * cubic)


def pack_halves(smoothed_ref, packed_ref):
    packed_ref[...] = pack(smoothed_ref[: CELLS // 2], smoothed_ref[CELLS // 2 :])


def unpack_row(packed_ref, i, upper):
    block = packed_ref[row_of(i)]
    return second_twin(block) if upper else first_twin(block)


def unpack_halves(packed_ref, target_ref):
    target_ref[: CELLS // 2] = first_twin(packed_ref[...])
    target_ref[CELLS // 2 :] = second_twin(packed_ref[...])


def every(ref, start, count):
    return ref[pl.ds(start, count, stride=2)]


def rows_loop(count, step, body):
    @pl.loop(0, count, step=step)
    def _(first):
        for part in range(step):
            body(first + part)


def turned_layer(arrived_ref, first_field, second_field, group):
    parts = [arrived_ref[pl.ds(8 * field + group, TILES, stride=24)] for field in (first_field, second_field)]
    return jnp.concatenate(parts, axis=0).T


def spread_kernel(arrived_ref, pair_ref):
    for group in range(8):
        pair_ref[group * LANES : (group + 1) * LANES] = turned_layer(arrived_ref, 0, 1, group)


def lateral_kernel(
    arrived_ref, pair_ref, gluing_ref, flips_ref, viscous_ref, velocity_ref, force_ref, conds_ref, image_ref,
    total_ref, faces_ref, viscous_pad, viscous_west, viscous_east, pad, west, east,
):
    gluing, flips = gluing_ref[...], flips_ref[...]
    viscous_ref[...] = first_twin(pair_ref[...])
    velocity_ref[...] = second_twin(pair_ref[...])
    viscous_pad[C : C + CELLS] = viscous_ref[...]
    pad[C : C + CELLS] = velocity_ref[...]
    fine_ghosts(viscous_pad, viscous_west, viscous_east, gluing, flips)
    fine_ghosts(pad, west, east, gluing, flips)

    def body(i):
        own, beside = lateral(viscous_pad, viscous_west, viscous_east, i)
        conds = [0.5 * (own + other) for other in beside]
        for direction in range(4):
            conds_ref[direction, row_of(i)] = conds[direction]
        image_ref[row_of(i)] = coupled(conds, lateral(pad, west, east, i)[1])
        total_ref[row_of(i)] = conds[0] + conds[1] + conds[2] + conds[3]

    rows_loop(C, 4, body)
    sums, wests = [], []
    for big in range(HALF):
        upper, lower = big * 2 * C, big * 2 * C + C
        cells = slice(big * HALF, (big + 1) * HALF)

        def both(ref, start):
            return every(ref, start, HALF) + every(ref, start + 1, HALF)

        def column(direction, start):
            ref = conds_ref.at[direction]
            return every(ref, upper + start, HALF) + every(ref, lower + start, HALF)

        faces = pack(both(conds_ref.at[1], lower), column(3, 1))
        for copy in range(CHIPS):
            faces_ref[copy, cells] = faces
        if big == 0:
            north = both(conds_ref.at[0], upper)
        wests.append(column(2, 0)[0:1])
        sums.append(both(viscous_ref, upper) + both(viscous_ref, lower))
    start = COARSE + COARSE // 2
    edge = pack(north, jnp.concatenate(wests, axis=0))
    for copy in range(CHIPS):
        for big in range(HALF // 2):
            first = COARSE + big * HALF
            faces_ref[copy, first : first + HALF] = pack(sums[big], sums[big + HALF // 2])
        faces_ref[copy, start : start + HALF] = edge
    for group in range(8):
        force_ref[group * LANES : (group + 1) * LANES] = turned_layer(arrived_ref, 2, 2, group)


def first_kernel(
    force_ref, viscous_ref, velocity_ref, lateral_ref, lateral_total_ref, above_ref, below_ref,
    radials_ref, total_ref, residual_ref, smoothed_ref, packed_ref,
):
    def body(i):
        here = row_of(i)
        viscous, velocity = viscous_ref[here], velocity_ref[here]
        beside = above_ref[here], below_ref[here]
        conds = [radial_weight * 0.5 * (viscous + first_twin(pair)) for pair in beside]
        cond_total = lateral_total_ref[here] + conds[0] + conds[1]
        radials_ref[0, here] = conds[0]
        radials_ref[1, here] = conds[1]
        total_ref[here] = cond_total
        image = lateral_ref[here] + conds[0] * second_twin(beside[0]) + conds[1] * second_twin(beside[1])
        smooth_row(i, force_ref[here], cond_total, velocity, image, residual_ref, smoothed_ref)

    rows_loop(C, 4, body)
    pack_halves(smoothed_ref, packed_ref)


def remain_kernel(
    conds_ref, radials_ref, total_ref, velocity_ref, residual_ref, smoothed_ref, above_ref, below_ref,
    gluing_ref, flips_ref, coarse_ref, pad, west, east, remain, damping,
):
    pad[C : C + CELLS] = smoothed_ref[...]
    fine_ghosts(pad, west, east, gluing_ref[...], flips_ref[...])
    for upper in range(2):
        offset = upper * (C // 2)

        def body(source, upper=upper, offset=offset):
            i = source + offset
            here = row_of(i)
            velocity = velocity_ref[here]
            damp = 3.0 * (cubic_weight * velocity * velocity)
            own, beside = lateral(pad, west, east, i)
            beside = beside + (unpack_row(above_ref, source, upper), unpack_row(below_ref, source, upper))
            conds = [conds_ref[direction, here] for direction in range(4)]
            conds += [radials_ref[direction, here] for direction in range(2)]
            image = (total_ref[here] + damp) * own - coupled(conds, beside)
            remain[here] = residual_ref[here] - image
            damping[here] = damp

        rows_loop(C // 2, 4, body)

    for big in range(HALF):
        sums = []
        for ref in (remain, damping):
            start = big * 2 * C
            sums.append(
                every(ref, start, HALF)
                + every(ref, start + 1, HALF)
                + every(ref, start + C, HALF)
                + every(ref, start + C + 1, HALF)
            )
        cells = slice(big * HALF, (big + 1) * HALF)
        sums = pack(sums[0], sums[1])
        for copy in range(CHIPS):
            coarse_ref[copy, cells] = sums


def for_core(place_ref, own_ref, other_ref, body):
    @pl.when(place_ref[0] % 2 == 0)
    def _():
        body(own_ref, other_ref)

    @pl.when(place_ref[0] % 2 == 1)
    def _():
        body(other_ref, own_ref)


def radial_pair(values):
    swapped = swap(values)
    shaped = swapped.reshape(values.shape[0] // 8, 8, LANES)
    before = pltpu.roll(shaped, 1, 1).reshape(values.shape)
    after = pltpu.roll(shaped, 7, 1).reshape(values.shape)
    return pack(swapped, after), pack(before, swapped)


def faces_kernel(
    place_ref, own_ref, other_ref, rows_ref, columns_ref, up_ref, down_ref, face_total_ref, sums
):
    middle, last = COARSE, COARSE + COARSE // 2
    half = COARSE // 2

    def arrange(even_ref, odd_ref):
        for sub in range(8):
            a, b = even_ref[sub, :middle], odd_ref[sub, :middle]
            rows_ref[pl.ds(LANES + sub, COARSE, stride=8)] = pack(a, swap(b))
            east = pack(swap(a), b)
            for big in range(HALF):
                columns_ref[big, pl.ds(8 + sub, HALF, stride=8)] = east[big * HALF : (big + 1) * HALF]
            a, b = even_ref[sub, middle:last], odd_ref[sub, middle:last]
            sums[pl.ds(sub, half, stride=8)] = pack(a, swap(b))
            sums[pl.ds(8 * half + sub, half, stride=8)] = pack(swap(a), b)
            a, b = even_ref[sub, last : last + HALF], odd_ref[sub, last : last + HALF]
            rows_ref[pl.ds(sub, HALF, stride=8)] = pack(a, swap(b))
            west = pack(swap(a), b)
            for big in range(HALF):
                columns_ref[big, sub : sub + 1] = west[big : big + 1]

    for_core(place_ref, own_ref, other_ref, arrange)
    side = HALF * 8
    shape = (side, LANES)
    row = lax.broadcasted_iota(jnp.int32, shape, 0) % 8
    lane = lax.broadcasted_iota(jnp.int32, shape, 1)
    top = (row == 7) & (lane >= TILES)
    bottom = (row == 0) & (lane < TILES)

    @pl.loop(0, HALF)
    def _(big):
        here = pl.ds(pl.multiple_of(big * side, side), side)
        own = sums[here]
        above, below = radial_pair(own)
        up = radial_weight * 0.5 * (own + jnp.where(top, 0.0, above))
        down = radial_weight * 0.5 * (own + jnp.where(bottom, 0.0, below))
        up_ref[here] = jnp.where(top, 0.0, up)
        down_ref[here] = jnp.where(bottom, 0.0, down)
        face_total_ref[here] = (
            rows_ref[here]
            + rows_ref[pl.ds(pl.multiple_of((big + 1) * side, side), side)]
            + columns_ref[big, :side]
            + columns_ref[big, 8 : 8 + side]
            + up
            + down
        )


def coarse_ghosts(pad, gluing, flips):
    side = HALF * 8
    inner = slice(8, 8 + side)
    north, south = pad[1, inner], pad[HALF, inner]
    west = pad[1 : HALF + 1, 8:16].reshape(side, LANES)
    east = pad[1 : HALF + 1, side : side + 8].reshape(side, LANES)
    first = jnp.concatenate([pack(north, swap(south)), pack(west, swap(east))], axis=1)
    second = jnp.concatenate([pack(swap(north), south), pack(swap(west), east)], axis=1)
    moved = glued(jnp.concatenate([first, second], axis=0), gluing)
    ghosts = []
    for pair in range(2):
        lanes = slice(pair * LANES, (pair + 1) * LANES)
        a, b = moved[:side, lanes], moved[side:, lanes]
        ghosts += [pack(a, swap(b)), pack(swap(a), b)]
    for number, ghost in enumerate(ghosts):
        flip = jnp.broadcast_to(flips[number : number + 1], (8, LANES)) > 0
        for k in range(HALF):
            other = HALF - 1 - k
            value = jnp.where(flip, ghost[8 * other : 8 * other + 8], ghost[8 * k : 8 * k + 8])
            if number < 2:
                pad[0 if number == 0 else HALF + 1, 8 + 8 * k : 16 + 8 * k] = value
            else:
                column = 0 if number == 2 else 8 + side
                pad[1 + k, column : column + 8] = value


def total_of(x):
    return jnp.sum(jnp.sum(x, axis=0, keepdims=True), axis=1, keepdims=True)


def folded(x):
    return jnp.sum(x.reshape(x.shape[0] // 8, 8, LANES), axis=0)


def solve_coarse(
    place_ref, own_ref, other_ref, rows_ref, columns_ref, up_ref, down_ref, face_total_ref, gluing, flips,
    pad, diagonal, image, residual, solution,
):
    side = HALF * 8
    inner = slice(8, 8 + side)
    chunk = 64

    def arrange(even_ref, odd_ref):
        for sub in range(8):
            a, b = even_ref[sub], odd_ref[sub]
            residual[pl.ds(sub, COARSE, stride=8)] = pack(a, swap(b))
            diagonal[pl.ds(sub, COARSE, stride=8)] = pack(swap(a), b)

    for_core(place_ref, own_ref, other_ref, arrange)
    zero = jnp.zeros((8, LANES), jnp.float32)

    def here_of(big):
        return pl.ds(pl.multiple_of(big * side, side), side)

    def total_over(body):
        def several(first, total):
            for part in range(4):
                total = body(first * 4 + part, total)
            return total

        return total_of(lax.fori_loop(0, HALF // 4, several, zero))

    def start(big, total):
        here = here_of(big)
        values = residual[here]
        pad[big + 1, inner] = values
        diagonal[here] = diagonal[here] + face_total_ref[here]
        return total + folded(values * values)

    norm = total_over(start)

    def apply_row(big, total):
        for part in range(side // chunk):
            first = part * chunk
            here = pl.ds(pl.multiple_of(big * side + first, chunk), chunk)
            own = pad[big + 1, 8 + first : 8 + first + chunk]
            above, below = radial_pair(own)
            south = pl.ds(pl.multiple_of((big + 1) * side + first, chunk), chunk)
            value = (
                rows_ref[here] * pad[big, 8 + first : 8 + first + chunk]
                + rows_ref[south] * pad[big + 2, 8 + first : 8 + first + chunk]
                + columns_ref[big, first : first + chunk] * pad[big + 1, first : first + chunk]
                + columns_ref[big, 8 + first : 8 + first + chunk] * pad[big + 1, 16 + first : 16 + first + chunk]
                + up_ref[here] * above
                + down_ref[here] * below
            )
            value = diagonal[here] * own - value
            image[here] = value
            total = total + folded(own * value)
        return total

    for step in range(CG_ITERS):
        coarse_ghosts(pad, gluing, flips)
        length = norm / total_over(apply_row)

        def advance(big, total, length=length, step=step):
            here = here_of(big)
            moved = length * pad[big + 1, inner]
            solution[here] = moved if step == 0 else solution[here] + moved
            if step + 1 == CG_ITERS:
                return total
            values = residual[here] - length * image[here]
            residual[here] = values
            return total + folded(values * values)

        following = total_over(advance)
        if step + 1 < CG_ITERS:
            ratio = following / norm
            norm = following

            def turn(big, total, ratio=ratio):
                pad[big + 1, inner] = residual[here_of(big)] + ratio * pad[big + 1, inner]
                return total

            total_over(turn)


def prolong_layer(solution, layer, target):
    inside = (layer >= 0) & (layer < NR)
    place = jnp.clip(layer, 0, NR - 1)
    values = solution[pl.ds(place // 2, COARSE, stride=8)]
    values = jnp.where(place % 2 == 0, first_twin(values), second_twin(values))
    values = jnp.where(inside, values, 0.0)
    for big in range(HALF):
        row = values[big * HALF : (big + 1) * HALF]
        for start in (0, 1, C, C + 1):
            target[pl.ds(big * 2 * C + start, HALF, stride=2)] = row


COARSE_SCRATCH = [
    pltpu.VMEM((HALF + 2, (HALF + 2) * 8, LANES), jnp.float32),
    *[pltpu.VMEM((COARSE * 8, LANES), jnp.float32) for _ in range(4)],
]


def step_kernel(
    place_ref, own_ref, other_ref, rows_ref, columns_ref, up_ref, down_ref, face_total_ref, gluing_ref, flips_ref,
    velocity_ref, above_ref, below_ref, smoothed_ref, smoothed_above_ref, smoothed_below_ref, force_ref,
    conds_ref, radials_ref, total_ref, new_velocity_ref, new_residual_ref, new_smoothed_ref, packed_ref,
    pad, diagonal, image, residual, solution, velocity, west, east, above, below, spread,
):
    gluing, flips = gluing_ref[...], flips_ref[...]
    for pairs, smooth, target in ((above_ref, smoothed_above_ref, above), (below_ref, smoothed_below_ref, below)):
        unpack_halves(smooth, target)
        target[...] = target[...] + second_twin(pairs[...])
    solve_coarse(
        place_ref, own_ref, other_ref, rows_ref, columns_ref, up_ref, down_ref, face_total_ref, gluing, flips,
        pad, diagonal, image, residual, solution,
    )
    layer = place_ref[0]
    prolong_layer(solution, layer, spread)
    velocity[C : C + CELLS] = velocity_ref[...] + smoothed_ref[...] + spread[...]
    new_velocity_ref[...] = velocity[C : C + CELLS]
    fine_ghosts(velocity, west, east, gluing, flips)
    for shift, target in ((1, above), (-1, below)):
        prolong_layer(solution, layer + shift, spread)
        target[...] = target[...] + spread[...]

    def body(i):
        here = row_of(i)
        own, beside = lateral(velocity, west, east, i)
        beside = beside + (above[here], below[here])
        conds = [conds_ref[direction, here] for direction in range(4)]
        conds += [radials_ref[direction, here] for direction in range(2)]
        smooth_row(i, force_ref[here], total_ref[here], own, coupled(conds, beside), new_residual_ref, new_smoothed_ref)

    rows_loop(C, 4, body)
    pack_halves(new_smoothed_ref, packed_ref)


def last_kernel(
    place_ref, own_ref, other_ref, rows_ref, columns_ref, up_ref, down_ref, face_total_ref, gluing_ref, flips_ref,
    velocity_ref, smoothed_ref, out_ref, pad, diagonal, image, residual, solution, spread, turned,
):
    solve_coarse(
        place_ref, own_ref, other_ref, rows_ref, columns_ref, up_ref, down_ref, face_total_ref,
        gluing_ref[...], flips_ref[...], pad, diagonal, image, residual, solution,
    )
    prolong_layer(solution, place_ref[0], spread)
    for group in range(8):
        cells = slice(group * LANES, (group + 1) * LANES)
        turned[cells] = (velocity_ref[cells] + smoothed_ref[cells] + spread[cells]).T
    for group in range(8):
        out_ref[group : group + 1] = turned[pl.ds(group * LANES + place_ref[1], 1)]


def call(kernel, outs, scratch, args, scalars=0, mebibytes=4):
    vmem = pl.BlockSpec(memory_space=pltpu.VMEM)
    shapes = [jax.ShapeDtypeStruct(shape, jnp.float32) for shape in outs]
    return pl.pallas_call(
        kernel,
        out_shape=shapes,
        in_specs=[pl.BlockSpec(memory_space=pltpu.SMEM)] * scalars + [vmem] * (len(args) - scalars),
        out_specs=[vmem] * len(outs),
        scratch_shapes=[pltpu.VMEM(shape, jnp.float32) for shape in scratch],
        compiler_params=pltpu.CompilerParams(vmem_limit_bytes=VMEM_MIB << 20),
        cost_estimate=pl.CostEstimate(flops=mebibytes << 20, bytes_accessed=mebibytes << 20, transcendentals=0),
    )(*args)


VMEM_MIB = 20
PADDED = (CELLS + 2 * C, LANES)
FINE = (CELLS, LANES)
PACKED = (CELLS // 2, LANES)
EDGE = (C, LANES)
FACES = (CHIPS, COARSE + COARSE // 2 + HALF, LANES)
GRID = (COARSE * 8, LANES)
COARSE_SCRATCH = [(HALF + 2, (HALF + 2) * 8, LANES)] + [GRID] * 4


def spread_layer(arrived):
    return call(spread_kernel, [FINE], [], [arrived])[0]


def lateral_stage(*args):
    outs = [FINE, FINE, FINE, (4,) + FINE, FINE, FINE, FACES]
    return call(lateral_kernel, outs, [PADDED, EDGE, EDGE, PADDED, EDGE, EDGE], args, mebibytes=24)


def first_stage(*args):
    return call(first_kernel, [(2,) + FINE, FINE, FINE, FINE, PACKED], [], args)


def remain_stage(*args):
    return call(remain_kernel, [(CHIPS, COARSE, LANES)], [PADDED, EDGE, EDGE, FINE, FINE], args)[0]


def faces_stage(*args):
    outs = [((HALF + 1) * HALF * 8, LANES), (HALF, (HALF + 1) * 8, LANES)] + [GRID] * 3
    return call(faces_kernel, outs, [GRID], args, 1, 24)


def step_stage(*args):
    scratch = COARSE_SCRATCH + [PADDED, EDGE, EDGE, FINE, FINE, FINE]
    return call(step_kernel, [FINE, FINE, FINE, PACKED], scratch, args, 1)


def last_stage(*args):
    return call(last_kernel, [(8, LANES)], COARSE_SCRATCH + [FINE, FINE], args, 1)[0]


NEAR = 4
FAR = TILES // NEAR


def place_of(tile):
    return tile // 2 % NEAR * FAR + tile // (2 * NEAR) * 2 + tile % 2


def gluing_tables(glue_tile, glue_side, glue_flip):
    def lanes_of(table):
        return table.reshape(FAR // 2, NEAR, 2, 4).transpose(3, 1, 0, 2).reshape(4, TILES)

    source = (lanes_of(glue_side) * TILES + place_of(lanes_of(glue_tile))).reshape(1, 4 * TILES)
    gluing = (jnp.arange(4 * TILES)[:, None] == source).astype(jnp.bfloat16)
    flips = lanes_of(glue_flip).astype(jnp.float32)
    flips = jnp.concatenate([flips, flips], axis=1)
    return gluing, jnp.concatenate([flips, flips], axis=0)


def gather(values, axis, groups):
    sent = jnp.broadcast_to(values[None], (len(groups[0]),) + values.shape)
    arrived = lax.all_to_all(sent, axis, split_axis=0, concat_axis=0, axis_index_groups=groups, tiled=True)
    return arrived.reshape((-1,) + values.shape[1:])


def gather_lateral(values):
    tiles = sorted(range(TILES), key=place_of)
    far = [tiles[near * FAR : (near + 1) * FAR] for near in range(NEAR)]
    return gather(gather(values, "lat", far), "lat", [list(group) for group in zip(*far)])


def gather_radial(copies):
    groups = [list(range(core, NR, 2)) for core in range(2)]
    own = lax.all_to_all(copies, "rad", split_axis=0, concat_axis=0, axis_index_groups=groups, tiled=True)
    other = lax.ppermute(own, "rad", [(layer, layer ^ 1) for layer in range(NR)])
    return own, other


def radial(values):
    backward = [(layer + 1, layer) for layer in range(NR - 1)]
    forward = [(layer, layer + 1) for layer in range(NR - 1)]
    return lax.ppermute(values, "rad", backward), lax.ppermute(values, "rad", forward)


def on_device(rhs_force, viscosity, initial_guess, glue_tile, glue_side, glue_flip):
    tables = gluing_tables(glue_tile, glue_side, glue_flip)
    place = jnp.stack([lax.axis_index("rad"), place_of(lax.axis_index("lat"))]).astype(jnp.int32)
    own = jnp.concatenate([field.reshape(8, LANES) for field in (viscosity, initial_guess, rhs_force)], axis=0)
    arrived = gather_lateral(own)
    pair = spread_layer(arrived)
    pair_beside = radial(pair)
    viscous, velocity, force, conds, lateral_image, lateral_total, faces = lateral_stage(arrived, pair, *tables)
    faces, *pair_beside = lax.optimization_barrier((faces, *pair_beside))
    radials, total, residual, smoothed, packed = first_stage(
        force, viscous, velocity, lateral_image, lateral_total, *pair_beside
    )
    smoothed_beside = radial(packed)
    coefficients = faces_stage(place, *gather_radial(faces))
    coarse = remain_stage(conds, radials, total, velocity, residual, smoothed, *smoothed_beside, *tables)
    velocity, residual, smoothed, packed = step_stage(
        place, *gather_radial(coarse), *coefficients, *tables, velocity, *pair_beside, smoothed,
        *smoothed_beside, force, conds, radials, total,
    )
    smoothed_beside = radial(packed)
    coarse = remain_stage(conds, radials, total, velocity, residual, smoothed, *smoothed_beside, *tables)
    out = last_stage(place, *gather_radial(coarse), *coefficients, *tables, velocity, smoothed)
    return out.reshape(1, CELLS)


def solution(mesh):
    return jax.shard_map(
        on_device,
        mesh=mesh,
        in_specs=(P("rad", "lat"), P("rad", "lat"), P("rad", "lat"), P(), P(), P()),
        out_specs=P("rad", "lat"),
        check_vma=False,
    )
```

```python
import math

import jax
import jax.numpy as jnp
from jax import lax
from jax.experimental import pallas as pl
from jax.experimental.pallas import tpu as pltpu
from jax.sharding import PartitionSpec as P

C = 32
HALF = 16
TILES = 64
NR = 16
CHIPS = NR // 2
CELLS = C * C
COARSE = HALF * HALF
LANES = 128
CG_ITERS = 4

cubic_weight = 8.0
radial_weight = 4.0
relax_factor = 0.8


def low(x):
    return lax.broadcasted_iota(jnp.int32, x.shape, x.ndim - 1) < TILES


def swap(x):
    return pltpu.roll(x, TILES, x.ndim - 1)


def pack(a, b):
    return jnp.where(low(a), a, b)


def first_twin(x):
    return jnp.where(low(x), x, swap(x))


def second_twin(x):
    return jnp.where(low(x), swap(x), x)


def twins(x):
    swapped = swap(x)
    return jnp.where(low(x), x, swapped), jnp.where(low(x), swapped, x)


def glued(values, gluing):
    rows = values.shape[0]
    high = values.astype(jnp.bfloat16)
    rest = values - high.astype(jnp.float32)
    middle = rest.astype(jnp.bfloat16)
    lowest = (rest - middle.astype(jnp.float32)).astype(jnp.bfloat16)
    moved = jnp.dot(
        jnp.concatenate([high, middle, lowest], axis=0), gluing, preferred_element_type=jnp.float32
    )
    return moved[:rows] + (moved[rows : 2 * rows] + moved[2 * rows :])


def fine_ghosts(pad_ref, west_ref, east_ref, gluing, flips):
    north, south = pad_ref[C : 2 * C], pad_ref[CELLS : CELLS + C]
    west, east = pad_ref[pl.ds(C, C, stride=C)], pad_ref[pl.ds(2 * C - 1, C, stride=C)]
    moved = glued(jnp.concatenate([pack(north, south), pack(west, east)], axis=1), gluing)
    mirror = lax.broadcasted_iota(jnp.int32, (C, C), 0) + lax.broadcasted_iota(jnp.int32, (C, C), 1) == C - 1
    mirrored = jnp.dot(
        mirror.astype(jnp.float32), moved, precision=lax.Precision.HIGHEST, preferred_element_type=jnp.float32
    )
    pairs = []
    for pair in range(2):
        lanes = slice(pair * LANES, (pair + 1) * LANES)
        flip = pack(flips[2 * pair : 2 * pair + 1], flips[2 * pair + 1 : 2 * pair + 2])
        pairs.append(jnp.where(flip > 0, mirrored[:, lanes], moved[:, lanes]))
    pad_ref[0:C] = first_twin(pairs[0])
    pad_ref[CELLS + C : CELLS + 2 * C] = second_twin(pairs[0])
    west_ref[...] = first_twin(pairs[1])
    east_ref[...] = second_twin(pairs[1])


def row_of(i):
    return pl.ds(pl.multiple_of(i * C, C), C)


def lateral(pad_ref, west_ref, east_ref, i):
    own = pad_ref[row_of(i + 1)]
    column = lax.broadcasted_iota(jnp.int32, own.shape, 0)
    west = jnp.where(column == 0, west_ref[pl.ds(i, 1)], pltpu.roll(own, 1, 0))
    east = jnp.where(column == C - 1, east_ref[pl.ds(i, 1)], pltpu.roll(own, C - 1, 0))
    return own, (pad_ref[row_of(i)], pad_ref[row_of(i + 2)], west, east)


def coupled(conds, beside):
    total = conds[0] * beside[0]
    for cond, value in zip(conds[1:], beside[1:]):
        total = total + cond * value
    return total


def smooth_row(i, force, cond_total, own, image, residual_ref, smoothed_ref):
    cubic = cubic_weight * own * own
    residual = force - ((cond_total + cubic) * own - image)
    residual_ref[row_of(i)] = residual
    smoothed_ref[row_of(i)] = relax_factor * residual / (cond_total + 3.0 * cubic)


def pack_halves(smoothed_ref, packed_ref):
    packed_ref[...] = pack(smoothed_ref[: CELLS // 2], smoothed_ref[CELLS // 2 :])


def unpack_row(packed_ref, i, upper):
    block = packed_ref[row_of(i)]
    return second_twin(block) if upper else first_twin(block)


def unpack_halves(packed_ref, target_ref):
    target_ref[: CELLS // 2] = first_twin(packed_ref[...])
    target_ref[CELLS // 2 :] = second_twin(packed_ref[...])


def every(ref, start, count):
    return ref[pl.ds(start, count, stride=2)]


def rows_loop(count, step, body):
    @pl.loop(0, count, step=step)
    def _(first):
        for part in range(step):
            body(first + part)


def turned_layer(arrived_ref, first_field, second_field, group):
    parts = [arrived_ref[pl.ds(8 * field + group, TILES, stride=24)] for field in (first_field, second_field)]
    return jnp.concatenate(parts, axis=0).T


def spread_kernel(ready, arrived_ref, pair_ref):
    for group in range(8):
        pair_ref[group * LANES : (group + 1) * LANES] = turned_layer(arrived_ref, 0, 1, group)


def lateral_kernel(
    ready, arrived_ref, pair_ref, gluing_ref, flips_ref, faces_ref, both_ref, rows_ref, columns_ref, lateral_ref,
    force_ref, viscous, conds, viscous_pad, viscous_west, viscous_east, pad, west, east,
):
    gluing, flips = gluing_ref[...], flips_ref[...]
    both_ref[...] = pair_ref[...]
    viscous[...] = first_twin(pair_ref[...])
    viscous_pad[C : C + CELLS] = viscous[...]
    pad[C : C + CELLS] = second_twin(pair_ref[...])
    fine_ghosts(viscous_pad, viscous_west, viscous_east, gluing, flips)
    fine_ghosts(pad, west, east, gluing, flips)

    def body(i):
        here = row_of(i)
        own, beside = lateral(viscous_pad, viscous_west, viscous_east, i)
        weights = [0.5 * (own + other) for other in beside]
        for direction in range(4):
            conds[direction, here] = weights[direction]
        rows_ref[here] = pack(weights[0], weights[1])
        columns_ref[here] = pack(weights[2], weights[3])
        image = coupled(weights, lateral(pad, west, east, i)[1])
        lateral_ref[here] = pack(image, weights[0] + weights[1] + weights[2] + weights[3])

    rows_loop(C, 4, body)
    sums, wests = [], []
    for big in range(HALF):
        upper, lower = big * 2 * C, big * 2 * C + C
        cells = slice(big * HALF, (big + 1) * HALF)

        def both(ref, start):
            return every(ref, start, HALF) + every(ref, start + 1, HALF)

        def column(direction, start):
            ref = conds.at[direction]
            return every(ref, upper + start, HALF) + every(ref, lower + start, HALF)

        faces = pack(both(conds.at[1], lower), column(3, 1))
        for copy in range(CHIPS):
            faces_ref[copy, cells] = faces
        if big == 0:
            north = both(conds.at[0], upper)
        wests.append(column(2, 0)[0:1])
        sums.append(both(viscous, upper) + both(viscous, lower))
    start = COARSE + COARSE // 2
    edge = pack(north, jnp.concatenate(wests, axis=0))
    for copy in range(CHIPS):
        for big in range(HALF // 2):
            first = COARSE + big * HALF
            faces_ref[copy, first : first + HALF] = pack(sums[big], sums[big + HALF // 2])
        faces_ref[copy, start : start + HALF] = edge
    for group in range(8):
        force_ref[group * LANES : (group + 1) * LANES] = turned_layer(arrived_ref, 2, 2, group)


def first_kernel(
    ready, above_ref, below_ref, pair_ref, lateral_ref, force_ref, packed_ref, radials_ref, total_ref, state_ref,
    residual, smoothed,
):
    ready()

    def body(i):
        here = row_of(i)
        own, lateral_sums = twins(pair_ref[here]), twins(lateral_ref[here])
        beside = twins(above_ref[here]), twins(below_ref[here])
        conds = [radial_weight * 0.5 * (own[0] + other[0]) for other in beside]
        cond_total = lateral_sums[1] + conds[0] + conds[1]
        radials_ref[here] = pack(conds[0], conds[1])
        total_ref[here] = pack(cond_total, force_ref[here])
        image = lateral_sums[0] + conds[0] * beside[0][1] + conds[1] * beside[1][1]
        smooth_row(i, force_ref[here], cond_total, own[1], image, residual, smoothed)
        state_ref[here] = pack(residual[here], smoothed[here])

    rows_loop(C, 4, body)
    pack_halves(smoothed, packed_ref)


def remain_kernel(
    ready, gluing_ref, flips_ref, above_ref, below_ref, state_ref, rows_ref, columns_ref, radials_ref, total_ref,
    velocity_ref, coarse_ref, pad, west, east, remain, damping,
):
    ready(0)
    pad[C : C + CELLS] = second_twin(state_ref[...])
    fine_ghosts(pad, west, east, gluing_ref[...], flips_ref[...])
    ready(*range(1, 6))
    for upper in range(2):
        offset = upper * (C // 2)

        def body(source, upper=upper, offset=offset):
            i = source + offset
            here = row_of(i)
            velocity = second_twin(velocity_ref[here])
            damp = 3.0 * (cubic_weight * velocity * velocity)
            own, beside = lateral(pad, west, east, i)
            beside = beside + (unpack_row(above_ref, source, upper), unpack_row(below_ref, source, upper))
            conds = twins(rows_ref[here]) + twins(columns_ref[here]) + twins(radials_ref[here])
            image = (first_twin(total_ref[here]) + damp) * own - coupled(conds, beside)
            remain[here] = first_twin(state_ref[here]) - image
            damping[here] = damp

        rows_loop(C // 2, 4, body)

    for big in range(HALF):
        sums = []
        for ref in (remain, damping):
            start = big * 2 * C
            sums.append(
                every(ref, start, HALF)
                + every(ref, start + 1, HALF)
                + every(ref, start + C, HALF)
                + every(ref, start + C + 1, HALF)
            )
        cells = slice(big * HALF, (big + 1) * HALF)
        sums = pack(sums[0], sums[1])
        for copy in range(CHIPS):
            coarse_ref[copy, cells] = sums


def for_core(place_ref, own_ref, other_ref, body):
    @pl.when(place_ref[0] % 2 == 0)
    def _():
        body(own_ref, other_ref)

    @pl.when(place_ref[0] % 2 == 1)
    def _():
        body(other_ref, own_ref)


def radial_pair(values):
    swapped = swap(values)
    shaped = swapped.reshape(values.shape[0] // 8, 8, LANES)
    before = pltpu.roll(shaped, 1, 1).reshape(values.shape)
    after = pltpu.roll(shaped, 7, 1).reshape(values.shape)
    return pack(swapped, after), pack(before, swapped)


def faces_kernel(
    ready, place_ref, own_ref, other_ref, rows_ref, columns_ref, up_ref, down_ref, face_total_ref, sums
):
    middle, last = COARSE, COARSE + COARSE // 2
    half = COARSE // 2

    def arrange(even_ref, odd_ref):
        for sub in range(8):
            a, b = even_ref[sub, :middle], odd_ref[sub, :middle]
            rows_ref[pl.ds(LANES + sub, COARSE, stride=8)] = pack(a, swap(b))
            east = pack(swap(a), b)
            for big in range(HALF):
                columns_ref[big, pl.ds(8 + sub, HALF, stride=8)] = east[big * HALF : (big + 1) * HALF]
            a, b = even_ref[sub, middle:last], odd_ref[sub, middle:last]
            sums[pl.ds(sub, half, stride=8)] = pack(a, swap(b))
            sums[pl.ds(8 * half + sub, half, stride=8)] = pack(swap(a), b)
            a, b = even_ref[sub, last : last + HALF], odd_ref[sub, last : last + HALF]
            rows_ref[pl.ds(sub, HALF, stride=8)] = pack(a, swap(b))
            west = pack(swap(a), b)
            for big in range(HALF):
                columns_ref[big, sub : sub + 1] = west[big : big + 1]

    for_core(place_ref, own_ref, other_ref, arrange)
    side = HALF * 8
    shape = (side, LANES)
    row = lax.broadcasted_iota(jnp.int32, shape, 0) % 8
    lane = lax.broadcasted_iota(jnp.int32, shape, 1)
    top = (row == 7) & (lane >= TILES)
    bottom = (row == 0) & (lane < TILES)

    @pl.loop(0, HALF)
    def _(big):
        here = pl.ds(pl.multiple_of(big * side, side), side)
        own = sums[here]
        above, below = radial_pair(own)
        up = radial_weight * 0.5 * (own + jnp.where(top, 0.0, above))
        down = radial_weight * 0.5 * (own + jnp.where(bottom, 0.0, below))
        up_ref[here] = jnp.where(top, 0.0, up)
        down_ref[here] = jnp.where(bottom, 0.0, down)
        face_total_ref[here] = (
            rows_ref[here]
            + rows_ref[pl.ds(pl.multiple_of((big + 1) * side, side), side)]
            + columns_ref[big, :side]
            + columns_ref[big, 8 : 8 + side]
            + up
            + down
        )


def coarse_ghosts(pad, gluing, flips):
    side = HALF * 8
    inner = slice(8, 8 + side)
    north, south = pad[1, inner], pad[HALF, inner]
    west = pad[1 : HALF + 1, 8:16].reshape(side, LANES)
    east = pad[1 : HALF + 1, side : side + 8].reshape(side, LANES)
    first = jnp.concatenate([pack(north, swap(south)), pack(west, swap(east))], axis=1)
    second = jnp.concatenate([pack(swap(north), south), pack(swap(west), east)], axis=1)
    moved = glued(jnp.concatenate([first, second], axis=0), gluing)
    ghosts = []
    for pair in range(2):
        lanes = slice(pair * LANES, (pair + 1) * LANES)
        a, b = moved[:side, lanes], moved[side:, lanes]
        ghosts += [pack(a, swap(b)), pack(swap(a), b)]
    for number, ghost in enumerate(ghosts):
        flip = jnp.broadcast_to(flips[number : number + 1], (8, LANES)) > 0
        for k in range(HALF):
            other = HALF - 1 - k
            value = jnp.where(flip, ghost[8 * other : 8 * other + 8], ghost[8 * k : 8 * k + 8])
            if number < 2:
                pad[0 if number == 0 else HALF + 1, 8 + 8 * k : 16 + 8 * k] = value
            else:
                column = 0 if number == 2 else 8 + side
                pad[1 + k, column : column + 8] = value


def total_of(x):
    return jnp.sum(jnp.sum(x, axis=0, keepdims=True), axis=1, keepdims=True)


def folded(x):
    return jnp.sum(x.reshape(x.shape[0] // 8, 8, LANES), axis=0)


def solve_coarse(
    place_ref, own_ref, other_ref, rows_ref, columns_ref, up_ref, down_ref, face_total_ref, gluing, flips,
    pad, diagonal, image, residual, solution,
):
    side = HALF * 8
    inner = slice(8, 8 + side)

    def arrange(even_ref, odd_ref):
        for sub in range(8):
            a, b = even_ref[sub], odd_ref[sub]
            residual[pl.ds(sub, COARSE, stride=8)] = pack(a, swap(b))
            diagonal[pl.ds(sub, COARSE, stride=8)] = pack(swap(a), b)

    for_core(place_ref, own_ref, other_ref, arrange)
    zero = jnp.zeros((8, LANES), jnp.float32)

    def here_of(big):
        return pl.ds(pl.multiple_of(big * side, side), side)

    def total_over(body):
        def several(first, total):
            for part in range(4):
                total = body(first * 4 + part, total)
            return total

        return total_of(lax.fori_loop(0, HALF // 4, several, zero))

    def start(big, total):
        here = here_of(big)
        values = residual[here]
        pad[big + 1, inner] = values
        diagonal[here] = diagonal[here] + face_total_ref[here]
        return total + folded(values * values)

    norm = total_over(start)

    def apply_row(big, total):
        here, south = here_of(big), here_of(big + 1)
        row, columns = pad[big + 1], columns_ref[big]
        own = row[inner]
        above, below = radial_pair(own)
        value = (
            rows_ref[here] * pad[big, inner]
            + rows_ref[south] * pad[big + 2, inner]
            + columns[:side] * row[:side]
            + columns[inner] * row[16 : 16 + side]
            + up_ref[here] * above
            + down_ref[here] * below
        )
        value = diagonal[here] * own - value
        image[here] = value
        return total + folded(own * value)

    for step in range(CG_ITERS):
        coarse_ghosts(pad, gluing, flips)
        length = norm / total_over(apply_row)

        def advance(big, total, length=length, step=step):
            here = here_of(big)
            moved = length * pad[big + 1, inner]
            solution[here] = moved if step == 0 else solution[here] + moved
            if step + 1 == CG_ITERS:
                return total
            values = residual[here] - length * image[here]
            residual[here] = values
            return total + folded(values * values)

        following = total_over(advance)
        if step + 1 < CG_ITERS:
            ratio = following / norm
            norm = following

            def turn(big, total, ratio=ratio):
                pad[big + 1, inner] = residual[here_of(big)] + ratio * pad[big + 1, inner]
                return total

            total_over(turn)


def prolong_layer(solution, layer, target):
    inside = (layer >= 0) & (layer < NR)
    place = jnp.clip(layer, 0, NR - 1)
    values = solution[pl.ds(place // 2, COARSE, stride=8)]
    values = jnp.where(place % 2 == 0, first_twin(values), second_twin(values))
    values = jnp.where(inside, values, 0.0)
    for big in range(HALF):
        row = values[big * HALF : (big + 1) * HALF]
        for start in (0, 1, C, C + 1):
            target[pl.ds(big * 2 * C + start, HALF, stride=2)] = row


COARSE_SCRATCH = [
    pltpu.VMEM((HALF + 2, (HALF + 2) * 8, LANES), jnp.float32),
    *[pltpu.VMEM((COARSE * 8, LANES), jnp.float32) for _ in range(4)],
]


def step_kernel(
    ready, place_ref, own_ref, other_ref, rows_ref, columns_ref, up_ref, down_ref, face_total_ref, gluing_ref,
    flips_ref, state_ref, smoothed_above_ref, smoothed_below_ref, fine_rows_ref, fine_columns_ref, radials_ref,
    total_ref, pair_ref, above_ref, below_ref, packed_ref, new_state_ref, new_velocity_ref,
    pad, diagonal, image, residual, solution, velocity, west, east, above, below, spread, fine_residual, smoothed,
):
    gluing, flips = gluing_ref[...], flips_ref[...]
    solve_coarse(
        place_ref, own_ref, other_ref, rows_ref, columns_ref, up_ref, down_ref, face_total_ref, gluing, flips,
        pad, diagonal, image, residual, solution,
    )
    ready()
    layer = place_ref[0]
    prolong_layer(solution, layer, spread)
    velocity[C : C + CELLS] = second_twin(pair_ref[...]) + second_twin(state_ref[...]) + spread[...]
    new_velocity_ref[...] = velocity[C : C + CELLS]
    fine_ghosts(velocity, west, east, gluing, flips)
    for shift, pairs, smooth, target in (
        (1, above_ref, smoothed_above_ref, above),
        (-1, below_ref, smoothed_below_ref, below),
    ):
        prolong_layer(solution, layer + shift, spread)
        unpack_halves(smooth, target)
        target[...] = second_twin(pairs[...]) + target[...] + spread[...]

    def body(i):
        here = row_of(i)
        own, beside = lateral(velocity, west, east, i)
        beside = beside + (above[here], below[here])
        conds = twins(fine_rows_ref[here]) + twins(fine_columns_ref[here]) + twins(radials_ref[here])
        cond_total, force = twins(total_ref[here])
        smooth_row(i, force, cond_total, own, coupled(conds, beside), fine_residual, smoothed)
        new_state_ref[here] = pack(fine_residual[here], smoothed[here])

    rows_loop(C, 4, body)
    pack_halves(smoothed, packed_ref)


def last_kernel(
    ready, place_ref, own_ref, other_ref, rows_ref, columns_ref, up_ref, down_ref, face_total_ref, gluing_ref,
    flips_ref, state_ref, velocity_ref, out_ref, pad, diagonal, image, residual, solution, spread, turned,
):
    solve_coarse(
        place_ref, own_ref, other_ref, rows_ref, columns_ref, up_ref, down_ref, face_total_ref,
        gluing_ref[...], flips_ref[...], pad, diagonal, image, residual, solution,
    )
    ready()
    prolong_layer(solution, place_ref[0], spread)
    for group in range(8):
        cells = slice(group * LANES, (group + 1) * LANES)
        turned[cells] = (velocity_ref[cells] + second_twin(state_ref[cells]) + spread[cells]).T
    for group in range(8):
        out_ref[group : group + 1] = turned[pl.ds(group * LANES + place_ref[1], 1)]


VMEM_BYTES = 24 << 20
CROWDED_BYTES = 125 << 19


def call(kernel, outs, scratch, args, scalars=0, fetched=0, stored=0, mebibytes=4, crowded=False):
    near_args, near_outs = len(args) - fetched, len(outs) - stored
    room = VMEM_BYTES
    if crowded:
        near_shapes = [arg.shape for arg in args[scalars:near_args]] + list(outs[:near_outs])
        room = CROWDED_BYTES - 4 * sum(math.prod(shape) for shape in near_shapes)
    far_shapes = [arg.shape for arg in args[near_args:]] + list(outs[near_outs:])

    def body(*refs):
        ins, results, rest = refs[: len(args)], refs[len(args) : len(args) + len(outs)], refs[len(args) + len(outs) :]
        semaphores, slots, rest = rest[0], rest[1 : 1 + len(far_shapes)], rest[1 + len(far_shapes) :]
        incoming = [
            pltpu.make_async_copy(ins[near_args + k], slots[k], semaphores.at[k]) for k in range(fetched)
        ]
        for copy in incoming:
            copy.start()

        def ready(*numbers):
            for number in numbers or range(fetched):
                incoming[number].wait()

        kernel(ready, *ins[:near_args], *slots[:fetched], *results[:near_outs], *slots[fetched:], *rest)
        outgoing = [
            pltpu.make_async_copy(slots[fetched + k], results[near_outs + k], semaphores.at[fetched + k])
            for k in range(stored)
        ]
        for copy in outgoing:
            copy.start()
        for copy in outgoing:
            copy.wait()

    def specs(near, far):
        return [pl.BlockSpec(memory_space=pltpu.VMEM)] * near + [pl.BlockSpec(memory_space=pltpu.HBM)] * far

    return pl.pallas_call(
        body,
        out_shape=[jax.ShapeDtypeStruct(shape, jnp.float32) for shape in outs],
        in_specs=[pl.BlockSpec(memory_space=pltpu.SMEM)] * scalars + specs(near_args - scalars, fetched),
        out_specs=specs(near_outs, stored),
        scratch_shapes=[pltpu.SemaphoreType.DMA((max(len(far_shapes), 1),))]
        + [pltpu.VMEM(shape, jnp.float32) for shape in far_shapes + scratch],
        compiler_params=pltpu.CompilerParams(vmem_limit_bytes=room),
        cost_estimate=pl.CostEstimate(flops=mebibytes << 20, bytes_accessed=mebibytes << 20, transcendentals=0),
        name=kernel.__name__,
    )(*args)


PADDED = (CELLS + 2 * C, LANES)
FINE = (CELLS, LANES)
PACKED = (CELLS // 2, LANES)
EDGE = (C, LANES)
FACES = (CHIPS, COARSE + COARSE // 2 + HALF, LANES)
GRID = (COARSE * 8, LANES)
COARSE_SCRATCH = [(HALF + 2, (HALF + 2) * 8, LANES)] + [GRID] * 4


def spread_layer(arrived):
    return call(spread_kernel, [FINE], [], [arrived])[0]


def lateral_stage(*args):
    scratch = [FINE, (4,) + FINE, PADDED, EDGE, EDGE, PADDED, EDGE, EDGE]
    return call(lateral_kernel, [FACES] + [FINE] * 5, scratch, args, stored=5, mebibytes=24, crowded=True)


def first_stage(*args):
    return call(first_kernel, [PACKED] + [FINE] * 3, [FINE, FINE], args, fetched=3, stored=3, crowded=True)


def remain_stage(*args, crowded):
    scratch = [PADDED, EDGE, EDGE, FINE, FINE]
    return call(remain_kernel, [(CHIPS, COARSE, LANES)], scratch, args, fetched=6, crowded=crowded)[0]


def faces_stage(*args):
    outs = [((HALF + 1) * HALF * 8, LANES), (HALF, (HALF + 1) * 8, LANES)] + [GRID] * 3
    return call(faces_kernel, outs, [GRID], args, 1, mebibytes=24)


def step_stage(*args):
    scratch = COARSE_SCRATCH + [PADDED, EDGE, EDGE] + [FINE] * 5
    return call(step_kernel, [PACKED, FINE, FINE], scratch, args, 1, fetched=10, stored=2)


def last_stage(*args):
    return call(last_kernel, [(8, LANES)], COARSE_SCRATCH + [FINE, FINE], args, 1, fetched=2)[0]


NEAR = 4
FAR = TILES // NEAR


def place_of(tile):
    return tile // 2 % NEAR * FAR + tile // (2 * NEAR) * 2 + tile % 2


def gluing_tables(glue_tile, glue_side, glue_flip):
    def lanes_of(table):
        return table.reshape(FAR // 2, NEAR, 2, 4).transpose(3, 1, 0, 2).reshape(4, TILES)

    source = (lanes_of(glue_side) * TILES + place_of(lanes_of(glue_tile))).reshape(1, 4 * TILES)
    gluing = (jnp.arange(4 * TILES)[:, None] == source).astype(jnp.bfloat16)
    flips = lanes_of(glue_flip).astype(jnp.float32)
    flips = jnp.concatenate([flips, flips], axis=1)
    return gluing, jnp.concatenate([flips, flips], axis=0)


def gather(values, axis, groups):
    sent = jnp.broadcast_to(values[None], (len(groups[0]),) + values.shape)
    arrived = lax.all_to_all(sent, axis, split_axis=0, concat_axis=0, axis_index_groups=groups, tiled=True)
    return arrived.reshape((-1,) + values.shape[1:])


def gather_lateral(values):
    tiles = sorted(range(TILES), key=place_of)
    far = [tiles[near * FAR : (near + 1) * FAR] for near in range(NEAR)]
    return gather(gather(values, "lat", far), "lat", [list(group) for group in zip(*far)])


def gather_radial(copies):
    groups = [list(range(core, NR, 2)) for core in range(2)]
    own = lax.all_to_all(copies, "rad", split_axis=0, concat_axis=0, axis_index_groups=groups, tiled=True)
    other = lax.ppermute(own, "rad", [(layer, layer ^ 1) for layer in range(NR)])
    return own, other


def radial(values):
    backward = [(layer + 1, layer) for layer in range(NR - 1)]
    forward = [(layer, layer + 1) for layer in range(NR - 1)]
    return lax.ppermute(values, "rad", backward), lax.ppermute(values, "rad", forward)


def on_device(rhs_force, viscosity, initial_guess, glue_tile, glue_side, glue_flip):
    tables = gluing_tables(glue_tile, glue_side, glue_flip)
    place = jnp.stack([lax.axis_index("rad"), place_of(lax.axis_index("lat"))]).astype(jnp.int32)
    own = jnp.concatenate([field.reshape(8, LANES) for field in (viscosity, initial_guess, rhs_force)], axis=0)
    arrived = gather_lateral(own)
    pair = spread_layer(arrived)
    beside = radial(pair)
    faces, pair, rows, columns, lateral_sums, force = lateral_stage(arrived, pair, *tables)
    faces, *beside = lax.optimization_barrier((faces, *beside))
    packed, radials, total, state = first_stage(*beside, pair, lateral_sums, force)
    smoothed_beside = radial(packed)
    coefficients = faces_stage(place, *gather_radial(faces))
    fine = rows, columns, radials, total
    coarse = remain_stage(*tables, *smoothed_beside, state, *fine, pair, crowded=True)
    packed, state, velocity = step_stage(
        place, *gather_radial(coarse), *coefficients, *tables, state, *smoothed_beside, *fine, pair, *beside
    )
    coarse = remain_stage(*tables, *radial(packed), state, *fine, velocity, crowded=False)
    out = last_stage(place, *gather_radial(coarse), *coefficients, *tables, state, velocity)
    return out.reshape(1, CELLS)


def solution(mesh):
    return jax.shard_map(
        on_device,
        mesh=mesh,
        in_specs=(P("rad", "lat"), P("rad", "lat"), P("rad", "lat"), P(), P(), P()),
        out_specs=P("rad", "lat"),
        check_vma=False,
    )
```

```python
import functools

import jax
import jax.numpy as jnp
from jax import lax
from jax.experimental import pallas as pl
from jax.experimental.pallas import tpu as pltpu
from jax.sharding import PartitionSpec as P

C = 32
HALF = 16
TILES = 64
NR = 16
CHIPS = NR // 2
CELLS = C * C
COARSE = HALF * HALF
LANES = 128
CG_ITERS = 4

cubic_weight = 8.0
radial_weight = 4.0
relax_factor = 0.8


def low(x):
    return lax.broadcasted_iota(jnp.int32, x.shape, x.ndim - 1) < TILES


def swap(x):
    return pltpu.roll(x, TILES, x.ndim - 1)


def pack(a, b):
    return jnp.where(low(a), a, b)


def first_twin(x):
    return jnp.where(low(x), x, swap(x))


def second_twin(x):
    return jnp.where(low(x), swap(x), x)


def glued(values, gluing):
    rows = values.shape[0]
    high = values.astype(jnp.bfloat16)
    rest = values - high.astype(jnp.float32)
    middle = rest.astype(jnp.bfloat16)
    lowest = (rest - middle.astype(jnp.float32)).astype(jnp.bfloat16)
    moved = jnp.dot(
        jnp.concatenate([high, middle, lowest], axis=0), gluing, preferred_element_type=jnp.float32
    )
    return moved[:rows] + (moved[rows : 2 * rows] + moved[2 * rows :])


def fine_ghosts(pad_ref, west_ref, east_ref, gluing, flips):
    north, south = pad_ref[C : 2 * C], pad_ref[CELLS : CELLS + C]
    west, east = pad_ref[pl.ds(C, C, stride=C)], pad_ref[pl.ds(2 * C - 1, C, stride=C)]
    moved = glued(jnp.concatenate([pack(north, south), pack(west, east)], axis=1), gluing)
    mirror = lax.broadcasted_iota(jnp.int32, (C, C), 0) + lax.broadcasted_iota(jnp.int32, (C, C), 1) == C - 1
    mirrored = jnp.dot(
        mirror.astype(jnp.float32), moved, precision=lax.Precision.HIGHEST, preferred_element_type=jnp.float32
    )
    pairs = []
    for pair in range(2):
        lanes = slice(pair * LANES, (pair + 1) * LANES)
        flip = pack(flips[2 * pair : 2 * pair + 1], flips[2 * pair + 1 : 2 * pair + 2])
        pairs.append(jnp.where(flip > 0, mirrored[:, lanes], moved[:, lanes]))
    pad_ref[0:C] = first_twin(pairs[0])
    pad_ref[CELLS + C : CELLS + 2 * C] = second_twin(pairs[0])
    west_ref[...] = first_twin(pairs[1])
    east_ref[...] = second_twin(pairs[1])


def row_of(i):
    return pl.ds(pl.multiple_of(i * C, C), C)


def lateral(pad_ref, west_ref, east_ref, i):
    own = pad_ref[row_of(i + 1)]
    column = lax.broadcasted_iota(jnp.int32, own.shape, 0)
    west = jnp.where(column == 0, west_ref[pl.ds(i, 1)], pltpu.roll(own, 1, 0))
    east = jnp.where(column == C - 1, east_ref[pl.ds(i, 1)], pltpu.roll(own, C - 1, 0))
    return own, (pad_ref[row_of(i)], pad_ref[row_of(i + 2)], west, east)


def coupled(conds, beside):
    total = conds[0] * beside[0]
    for cond, value in zip(conds[1:], beside[1:]):
        total = total + cond * value
    return total


def smooth_row(i, force, cond_total, own, image, residual_ref, smoothed_ref):
    cubic = cubic_weight * own * own
    residual = force - ((cond_total + cubic) * own - image)
    residual_ref[row_of(i)] = residual
    smoothed_ref[row_of(i)] = relax_factor * residual / (cond_total + 3.0 * cubic)


def pack_halves(smoothed_ref, packed_ref):
    packed_ref[...] = pack(smoothed_ref[: CELLS // 2], smoothed_ref[CELLS // 2 :])


def unpack_row(packed_ref, i, upper):
    block = packed_ref[row_of(i)]
    return second_twin(block) if upper else first_twin(block)


def unpack_halves(packed_ref, target_ref):
    target_ref[: CELLS // 2] = first_twin(packed_ref[...])
    target_ref[CELLS // 2 :] = second_twin(packed_ref[...])


def every(ref, start, count):
    return ref[pl.ds(start, count, stride=2)]


def rows_loop(count, step, body):
    @pl.loop(0, count, step=step)
    def _(first):
        for part in range(step):
            body(first + part)


def turned_layer(arrived_ref, first_field, second_field, group):
    parts = [arrived_ref[pl.ds(8 * field + group, TILES, stride=24)] for field in (first_field, second_field)]
    return jnp.concatenate(parts, axis=0).T


def spread_kernel(arrived_ref, pair_ref):
    for group in range(8):
        pair_ref[group * LANES : (group + 1) * LANES] = turned_layer(arrived_ref, 0, 1, group)


def lateral_kernel(
    arrived_ref, pair_ref, gluing_ref, flips_ref, viscous_ref, velocity_ref, force_ref, conds_ref, image_ref,
    total_ref, faces_ref, viscous_pad, viscous_west, viscous_east, pad, west, east,
):
    gluing, flips = gluing_ref[...], flips_ref[...]
    viscous_ref[...] = first_twin(pair_ref[...])
    velocity_ref[...] = second_twin(pair_ref[...])
    viscous_pad[C : C + CELLS] = viscous_ref[...]
    pad[C : C + CELLS] = velocity_ref[...]
    fine_ghosts(viscous_pad, viscous_west, viscous_east, gluing, flips)
    fine_ghosts(pad, west, east, gluing, flips)

    def body(i):
        own, beside = lateral(viscous_pad, viscous_west, viscous_east, i)
        conds = [0.5 * (own + other) for other in beside]
        for direction in range(4):
            conds_ref[direction, row_of(i)] = conds[direction]
        image_ref[row_of(i)] = coupled(conds, lateral(pad, west, east, i)[1])
        total_ref[row_of(i)] = conds[0] + conds[1] + conds[2] + conds[3]

    rows_loop(C, 4, body)
    sums, wests = [], []
    for big in range(HALF):
        upper, lower = big * 2 * C, big * 2 * C + C
        cells = slice(big * HALF, (big + 1) * HALF)

        def both(ref, start):
            return every(ref, start, HALF) + every(ref, start + 1, HALF)

        def column(direction, start):
            ref = conds_ref.at[direction]
            return every(ref, upper + start, HALF) + every(ref, lower + start, HALF)

        faces = pack(both(conds_ref.at[1], lower), column(3, 1))
        for copy in range(CHIPS):
            faces_ref[copy, cells] = faces
        if big == 0:
            north = both(conds_ref.at[0], upper)
        wests.append(column(2, 0)[0:1])
        sums.append(both(viscous_ref, upper) + both(viscous_ref, lower))
    start = COARSE + COARSE // 2
    edge = pack(north, jnp.concatenate(wests, axis=0))
    for copy in range(CHIPS):
        for big in range(HALF // 2):
            first = COARSE + big * HALF
            faces_ref[copy, first : first + HALF] = pack(sums[big], sums[big + HALF // 2])
        faces_ref[copy, start : start + HALF] = edge
    for group in range(8):
        force_ref[group * LANES : (group + 1) * LANES] = turned_layer(arrived_ref, 2, 2, group)


def first_kernel(
    force_ref, viscous_ref, velocity_ref, lateral_ref, lateral_total_ref, above_ref, below_ref,
    radials_ref, total_ref, residual_ref, smoothed_ref, packed_ref,
):
    def body(i):
        here = row_of(i)
        viscous, velocity = viscous_ref[here], velocity_ref[here]
        beside = above_ref[here], below_ref[here]
        conds = [radial_weight * 0.5 * (viscous + first_twin(pair)) for pair in beside]
        cond_total = lateral_total_ref[here] + conds[0] + conds[1]
        radials_ref[0, here] = conds[0]
        radials_ref[1, here] = conds[1]
        total_ref[here] = cond_total
        image = lateral_ref[here] + conds[0] * second_twin(beside[0]) + conds[1] * second_twin(beside[1])
        smooth_row(i, force_ref[here], cond_total, velocity, image, residual_ref, smoothed_ref)

    rows_loop(C, 4, body)
    pack_halves(smoothed_ref, packed_ref)


def remain_kernel(
    conds_ref, radials_ref, total_ref, velocity_ref, residual_ref, smoothed_ref, above_ref, below_ref,
    gluing_ref, flips_ref, coarse_ref, pad, west, east, remain, damping,
):
    pad[C : C + CELLS] = smoothed_ref[...]
    fine_ghosts(pad, west, east, gluing_ref[...], flips_ref[...])
    for upper in range(2):
        offset = upper * (C // 2)

        def body(source, upper=upper, offset=offset):
            i = source + offset
            here = row_of(i)
            velocity = velocity_ref[here]
            damp = 3.0 * (cubic_weight * velocity * velocity)
            own, beside = lateral(pad, west, east, i)
            beside = beside + (unpack_row(above_ref, source, upper), unpack_row(below_ref, source, upper))
            conds = [conds_ref[direction, here] for direction in range(4)]
            conds += [radials_ref[direction, here] for direction in range(2)]
            image = (total_ref[here] + damp) * own - coupled(conds, beside)
            remain[here] = residual_ref[here] - image
            damping[here] = damp

        rows_loop(C // 2, 4, body)

    for big in range(HALF):
        sums = []
        for ref in (remain, damping):
            start = big * 2 * C
            sums.append(
                every(ref, start, HALF)
                + every(ref, start + 1, HALF)
                + every(ref, start + C, HALF)
                + every(ref, start + C + 1, HALF)
            )
        cells = slice(big * HALF, (big + 1) * HALF)
        sums = pack(sums[0], sums[1])
        for copy in range(CHIPS):
            coarse_ref[copy, cells] = sums


def for_core(place_ref, own_ref, other_ref, body):
    @pl.when(place_ref[0] % 2 == 0)
    def _():
        body(own_ref, other_ref)

    @pl.when(place_ref[0] % 2 == 1)
    def _():
        body(other_ref, own_ref)


def radial_pair(values):
    swapped = swap(values)
    shaped = swapped.reshape(values.shape[0] // 8, 8, LANES)
    before = pltpu.roll(shaped, 1, 1).reshape(values.shape)
    after = pltpu.roll(shaped, 7, 1).reshape(values.shape)
    return pack(swapped, after), pack(before, swapped)


def faces_kernel(
    place_ref, own_ref, other_ref, rows_ref, columns_ref, up_ref, down_ref, face_total_ref, sums
):
    middle, last = COARSE, COARSE + COARSE // 2
    half = COARSE // 2

    def arrange(even_ref, odd_ref):
        for sub in range(8):
            a, b = even_ref[sub, :middle], odd_ref[sub, :middle]
            rows_ref[pl.ds(LANES + sub, COARSE, stride=8)] = pack(a, swap(b))
            east = pack(swap(a), b)
            for big in range(HALF):
                columns_ref[big, pl.ds(8 + sub, HALF, stride=8)] = east[big * HALF : (big + 1) * HALF]
            a, b = even_ref[sub, middle:last], odd_ref[sub, middle:last]
            sums[pl.ds(sub, half, stride=8)] = pack(a, swap(b))
            sums[pl.ds(8 * half + sub, half, stride=8)] = pack(swap(a), b)
            a, b = even_ref[sub, last : last + HALF], odd_ref[sub, last : last + HALF]
            rows_ref[pl.ds(sub, HALF, stride=8)] = pack(a, swap(b))
            west = pack(swap(a), b)
            for big in range(HALF):
                columns_ref[big, sub : sub + 1] = west[big : big + 1]

    for_core(place_ref, own_ref, other_ref, arrange)
    side = HALF * 8
    shape = (side, LANES)
    row = lax.broadcasted_iota(jnp.int32, shape, 0) % 8
    lane = lax.broadcasted_iota(jnp.int32, shape, 1)
    top = (row == 7) & (lane >= TILES)
    bottom = (row == 0) & (lane < TILES)

    @pl.loop(0, HALF)
    def _(big):
        here = pl.ds(pl.multiple_of(big * side, side), side)
        own = sums[here]
        above, below = radial_pair(own)
        up = radial_weight * 0.5 * (own + jnp.where(top, 0.0, above))
        down = radial_weight * 0.5 * (own + jnp.where(bottom, 0.0, below))
        up_ref[here] = jnp.where(top, 0.0, up)
        down_ref[here] = jnp.where(bottom, 0.0, down)
        face_total_ref[here] = (
            rows_ref[here]
            + rows_ref[pl.ds(pl.multiple_of((big + 1) * side, side), side)]
            + columns_ref[big, :side]
            + columns_ref[big, 8 : 8 + side]
            + up
            + down
        )


def coarse_ghosts(pad, gluing, flips):
    side = HALF * 8
    inner = slice(8, 8 + side)
    north, south = pad[1, inner], pad[HALF, inner]
    west = pad[1 : HALF + 1, 8:16].reshape(side, LANES)
    east = pad[1 : HALF + 1, side : side + 8].reshape(side, LANES)
    first = jnp.concatenate([pack(north, swap(south)), pack(west, swap(east))], axis=1)
    second = jnp.concatenate([pack(swap(north), south), pack(swap(west), east)], axis=1)
    moved = glued(jnp.concatenate([first, second], axis=0), gluing)
    ghosts = []
    for pair in range(2):
        lanes = slice(pair * LANES, (pair + 1) * LANES)
        a, b = moved[:side, lanes], moved[side:, lanes]
        ghosts += [pack(a, swap(b)), pack(swap(a), b)]
    for number, ghost in enumerate(ghosts):
        flip = jnp.broadcast_to(flips[number : number + 1], (8, LANES)) > 0
        for k in range(HALF):
            other = HALF - 1 - k
            value = jnp.where(flip, ghost[8 * other : 8 * other + 8], ghost[8 * k : 8 * k + 8])
            if number < 2:
                pad[0 if number == 0 else HALF + 1, 8 + 8 * k : 16 + 8 * k] = value
            else:
                column = 0 if number == 2 else 8 + side
                pad[1 + k, column : column + 8] = value


def total_of(x):
    return jnp.sum(jnp.sum(x, axis=0, keepdims=True), axis=1, keepdims=True)


def folded(x):
    return jnp.sum(x.reshape(x.shape[0] // 8, 8, LANES), axis=0)


def solve_coarse(
    place_ref, own_ref, other_ref, rows_ref, columns_ref, up_ref, down_ref, face_total_ref, gluing, flips,
    pad, diagonal, image, residual, solution,
):
    side = HALF * 8
    inner = slice(8, 8 + side)
    chunk = 64

    def arrange(even_ref, odd_ref):
        for sub in range(8):
            a, b = even_ref[sub], odd_ref[sub]
            residual[pl.ds(sub, COARSE, stride=8)] = pack(a, swap(b))
            diagonal[pl.ds(sub, COARSE, stride=8)] = pack(swap(a), b)

    for_core(place_ref, own_ref, other_ref, arrange)
    zero = jnp.zeros((8, LANES), jnp.float32)

    def here_of(big):
        return pl.ds(pl.multiple_of(big * side, side), side)

    def total_over(body):
        def several(first, total):
            for part in range(4):
                total = body(first * 4 + part, total)
            return total

        return total_of(lax.fori_loop(0, HALF // 4, several, zero))

    def start(big, total):
        here = here_of(big)
        values = residual[here]
        pad[big + 1, inner] = values
        diagonal[here] = diagonal[here] + face_total_ref[here]
        return total + folded(values * values)

    norm = total_over(start)

    def apply_row(big, total):
        for part in range(side // chunk):
            first = part * chunk
            here = pl.ds(pl.multiple_of(big * side + first, chunk), chunk)
            own = pad[big + 1, 8 + first : 8 + first + chunk]
            above, below = radial_pair(own)
            south = pl.ds(pl.multiple_of((big + 1) * side + first, chunk), chunk)
            value = (
                rows_ref[here] * pad[big, 8 + first : 8 + first + chunk]
                + rows_ref[south] * pad[big + 2, 8 + first : 8 + first + chunk]
                + columns_ref[big, first : first + chunk] * pad[big + 1, first : first + chunk]
                + columns_ref[big, 8 + first : 8 + first + chunk] * pad[big + 1, 16 + first : 16 + first + chunk]
                + up_ref[here] * above
                + down_ref[here] * below
            )
            value = diagonal[here] * own - value
            image[here] = value
            total = total + folded(own * value)
        return total

    for step in range(CG_ITERS):
        coarse_ghosts(pad, gluing, flips)
        length = norm / total_over(apply_row)

        def advance(big, total, length=length, step=step):
            here = here_of(big)
            moved = length * pad[big + 1, inner]
            solution[here] = moved if step == 0 else solution[here] + moved
            if step + 1 == CG_ITERS:
                return total
            values = residual[here] - length * image[here]
            residual[here] = values
            return total + folded(values * values)

        following = total_over(advance)
        if step + 1 < CG_ITERS:
            ratio = following / norm
            norm = following

            def turn(big, total, ratio=ratio):
                pad[big + 1, inner] = residual[here_of(big)] + ratio * pad[big + 1, inner]
                return total

            total_over(turn)


def prolong_layer(solution, layer, target):
    inside = (layer >= 0) & (layer < NR)
    place = jnp.clip(layer, 0, NR - 1)
    values = solution[pl.ds(place // 2, COARSE, stride=8)]
    values = jnp.where(place % 2 == 0, first_twin(values), second_twin(values))
    values = jnp.where(inside, values, 0.0)
    for big in range(HALF):
        row = values[big * HALF : (big + 1) * HALF]
        for start in (0, 1, C, C + 1):
            target[pl.ds(big * 2 * C + start, HALF, stride=2)] = row


COARSE_SCRATCH = [
    pltpu.VMEM((HALF + 2, (HALF + 2) * 8, LANES), jnp.float32),
    *[pltpu.VMEM((COARSE * 8, LANES), jnp.float32) for _ in range(4)],
]


def step_kernel(
    place_ref, own_ref, other_ref, rows_ref, columns_ref, up_ref, down_ref, face_total_ref, gluing_ref, flips_ref,
    velocity_ref, above_ref, below_ref, smoothed_ref, smoothed_above_ref, smoothed_below_ref, force_ref,
    conds_ref, radials_ref, total_ref, new_velocity_ref, new_residual_ref, new_smoothed_ref, packed_ref,
    pad, diagonal, image, residual, solution, velocity, west, east, above, below, spread,
):
    gluing, flips = gluing_ref[...], flips_ref[...]
    for pairs, smooth, target in ((above_ref, smoothed_above_ref, above), (below_ref, smoothed_below_ref, below)):
        unpack_halves(smooth, target)
        target[...] = target[...] + second_twin(pairs[...])
    solve_coarse(
        place_ref, own_ref, other_ref, rows_ref, columns_ref, up_ref, down_ref, face_total_ref, gluing, flips,
        pad, diagonal, image, residual, solution,
    )
    layer = place_ref[0]
    prolong_layer(solution, layer, spread)
    velocity[C : C + CELLS] = velocity_ref[...] + smoothed_ref[...] + spread[...]
    new_velocity_ref[...] = velocity[C : C + CELLS]
    fine_ghosts(velocity, west, east, gluing, flips)
    for shift, target in ((1, above), (-1, below)):
        prolong_layer(solution, layer + shift, spread)
        target[...] = target[...] + spread[...]

    def body(i):
        here = row_of(i)
        own, beside = lateral(velocity, west, east, i)
        beside = beside + (above[here], below[here])
        conds = [conds_ref[direction, here] for direction in range(4)]
        conds += [radials_ref[direction, here] for direction in range(2)]
        smooth_row(i, force_ref[here], total_ref[here], own, coupled(conds, beside), new_residual_ref, new_smoothed_ref)

    rows_loop(C, 4, body)
    pack_halves(new_smoothed_ref, packed_ref)


def last_kernel(
    place_ref, own_ref, other_ref, rows_ref, columns_ref, up_ref, down_ref, face_total_ref, gluing_ref, flips_ref,
    velocity_ref, smoothed_ref, out_ref, pad, diagonal, image, residual, solution, spread, turned,
):
    solve_coarse(
        place_ref, own_ref, other_ref, rows_ref, columns_ref, up_ref, down_ref, face_total_ref,
        gluing_ref[...], flips_ref[...], pad, diagonal, image, residual, solution,
    )
    prolong_layer(solution, place_ref[0], spread)
    for group in range(8):
        cells = slice(group * LANES, (group + 1) * LANES)
        turned[cells] = (velocity_ref[cells] + smoothed_ref[cells] + spread[cells]).T
    for group in range(8):
        out_ref[group : group + 1] = turned[pl.ds(group * LANES + place_ref[1], 1)]


def call(kernel, outs, scratch, args, scalars=0, mebibytes=4):
    vmem = pl.BlockSpec(memory_space=pltpu.VMEM)
    shapes = [jax.ShapeDtypeStruct(shape, jnp.float32) for shape in outs]
    return pl.pallas_call(
        kernel,
        out_shape=shapes,
        in_specs=[pl.BlockSpec(memory_space=pltpu.SMEM)] * scalars + [vmem] * (len(args) - scalars),
        out_specs=[vmem] * len(outs),
        scratch_shapes=[pltpu.VMEM(shape, jnp.float32) for shape in scratch],
        compiler_params=pltpu.CompilerParams(vmem_limit_bytes=VMEM_MIB << 20),
        cost_estimate=pl.CostEstimate(flops=mebibytes << 20, bytes_accessed=mebibytes << 20, transcendentals=0),
    )(*args)


VMEM_MIB = 20
PADDED = (CELLS + 2 * C, LANES)
FINE = (CELLS, LANES)
PACKED = (CELLS // 2, LANES)
EDGE = (C, LANES)
FACES = (CHIPS, COARSE + COARSE // 2 + HALF, LANES)
GRID = (COARSE * 8, LANES)
COARSE_SCRATCH = [(HALF + 2, (HALF + 2) * 8, LANES)] + [GRID] * 4


def spread_layer(arrived):
    return call(spread_kernel, [FINE], [], [arrived])[0]


def lateral_stage(*args):
    outs = [FINE, FINE, FINE, (4,) + FINE, FINE, FINE, FACES]
    return call(lateral_kernel, outs, [PADDED, EDGE, EDGE, PADDED, EDGE, EDGE], args, mebibytes=24)


def first_stage(*args):
    return call(first_kernel, [(2,) + FINE, FINE, FINE, FINE, PACKED], [], args)


def remain_stage(*args):
    return call(remain_kernel, [(CHIPS, COARSE, LANES)], [PADDED, EDGE, EDGE, FINE, FINE], args)[0]


def faces_stage(*args):
    outs = [((HALF + 1) * HALF * 8, LANES), (HALF, (HALF + 1) * 8, LANES)] + [GRID] * 3
    return call(faces_kernel, outs, [GRID], args, 1, 24)


def step_stage(*args):
    scratch = COARSE_SCRATCH + [PADDED, EDGE, EDGE, FINE, FINE, FINE]
    return call(step_kernel, [FINE, FINE, FINE, PACKED], scratch, args, 1)


def last_stage(*args):
    return call(last_kernel, [(8, LANES)], COARSE_SCRATCH + [FINE, FINE], args, 1)[0]


NEAR = 4
FAR = TILES // NEAR


def place_of(tile):
    return tile // 2 % NEAR * FAR + tile // (2 * NEAR) * 2 + tile % 2


def gluing_tables(glue_tile, glue_side, glue_flip):
    def lanes_of(table):
        return table.reshape(FAR // 2, NEAR, 2, 4).transpose(3, 1, 0, 2).reshape(4, TILES)

    source = (lanes_of(glue_side) * TILES + place_of(lanes_of(glue_tile))).reshape(1, 4 * TILES)
    gluing = (jnp.arange(4 * TILES)[:, None] == source).astype(jnp.bfloat16)
    flips = lanes_of(glue_flip).astype(jnp.float32)
    flips = jnp.concatenate([flips, flips], axis=1)
    return gluing, jnp.concatenate([flips, flips], axis=0)


def gather(values, axis, groups):
    sent = jnp.broadcast_to(values[None], (len(groups[0]),) + values.shape)
    arrived = lax.all_to_all(sent, axis, split_axis=0, concat_axis=0, axis_index_groups=groups, tiled=True)
    return arrived.reshape((-1,) + values.shape[1:])


def gather_lateral(values):
    tiles = sorted(range(TILES), key=place_of)
    far = [tiles[near * FAR : (near + 1) * FAR] for near in range(NEAR)]
    return gather(gather(values, "lat", far), "lat", [list(group) for group in zip(*far)])


def gather_cores(copies):
    groups = [list(range(core, NR, 2)) for core in range(2)]
    return lax.all_to_all(copies, "rad", split_axis=0, concat_axis=0, axis_index_groups=groups, tiled=True)


def swap_cores(own):
    return lax.ppermute(own, "rad", [(layer, layer ^ 1) for layer in range(NR)])


def gather_radial(copies):
    own = gather_cores(copies)
    return own, swap_cores(own)


def radial(values):
    backward = [(layer + 1, layer) for layer in range(NR - 1)]
    forward = [(layer, layer + 1) for layer in range(NR - 1)]
    return lax.ppermute(values, "rad", backward), lax.ppermute(values, "rad", forward)


def on_device(rhs_force, viscosity, initial_guess, glue_tile, glue_side, glue_flip):
    tables = gluing_tables(glue_tile, glue_side, glue_flip)
    place = jnp.stack([lax.axis_index("rad"), place_of(lax.axis_index("lat"))]).astype(jnp.int32)
    own = jnp.concatenate([field.reshape(8, LANES) for field in (viscosity, initial_guess, rhs_force)], axis=0)
    own, place = lax.optimization_barrier((own, place))
    arrived = gather_lateral(own)
    pair = spread_layer(arrived)
    pair_beside = radial(pair)
    viscous, velocity, force, conds, lateral_image, lateral_total, faces = lateral_stage(arrived, pair, *tables)
    faces, *pair_beside = lax.optimization_barrier((faces, *pair_beside))
    faces_gathered, *pair_beside = lax.optimization_barrier((gather_cores(faces), *pair_beside))
    faces_swapped = swap_cores(faces_gathered)
    radials, total, residual, smoothed, packed = first_stage(
        force, viscous, velocity, lateral_image, lateral_total, *pair_beside
    )
    coefficients = faces_stage(place, faces_gathered, faces_swapped)
    *smoothed_beside, coefficients = lax.optimization_barrier((*radial(packed), coefficients))
    coarse = remain_stage(conds, radials, total, velocity, residual, smoothed, *smoothed_beside, *tables)
    velocity, residual, smoothed, packed = step_stage(
        place, *gather_radial(coarse), *coefficients, *tables, velocity, *pair_beside, smoothed,
        *smoothed_beside, force, conds, radials, total,
    )
    smoothed_beside = radial(packed)
    coarse = remain_stage(conds, radials, total, velocity, residual, smoothed, *smoothed_beside, *tables)
    out = last_stage(place, *gather_radial(coarse), *coefficients, *tables, velocity, smoothed)
    return out.reshape(1, CELLS)


def solution(mesh):
    return jax.shard_map(
        on_device,
        mesh=mesh,
        in_specs=(P("rad", "lat"), P("rad", "lat"), P("rad", "lat"), P(), P(), P()),
        out_specs=P("rad", "lat"),
        check_vma=False,
    )
```

```python
import functools

import jax
import jax.numpy as jnp
from jax import lax
from jax.experimental import pallas as pl
from jax.experimental.pallas import tpu as pltpu
from jax.sharding import PartitionSpec as P

C = 32
HALF = 16
TILES = 64
NR = 16
CHIPS = NR // 2
CELLS = C * C
COARSE = HALF * HALF
LANES = 128
CG_ITERS = 4

cubic_weight = 8.0
radial_weight = 4.0
relax_factor = 0.8


def low(x):
    return lax.broadcasted_iota(jnp.int32, x.shape, x.ndim - 1) < TILES


def swap(x):
    return pltpu.roll(x, TILES, x.ndim - 1)


def pack(a, b):
    return jnp.where(low(a), a, b)


def first_twin(x):
    return jnp.where(low(x), x, swap(x))


def second_twin(x):
    return jnp.where(low(x), swap(x), x)


def glued(values, gluing):
    rows = values.shape[0]
    high = values.astype(jnp.bfloat16)
    rest = values - high.astype(jnp.float32)
    middle = rest.astype(jnp.bfloat16)
    lowest = (rest - middle.astype(jnp.float32)).astype(jnp.bfloat16)
    moved = jnp.dot(
        jnp.concatenate([high, middle, lowest], axis=0), gluing, preferred_element_type=jnp.float32
    )
    return moved[:rows] + (moved[rows : 2 * rows] + moved[2 * rows :])


def fine_ghosts(pad_ref, west_ref, east_ref, gluing, flips):
    north, south = pad_ref[C : 2 * C], pad_ref[CELLS : CELLS + C]
    west, east = pad_ref[pl.ds(C, C, stride=C)], pad_ref[pl.ds(2 * C - 1, C, stride=C)]
    moved = glued(jnp.concatenate([pack(north, south), pack(west, east)], axis=1), gluing)
    mirror = lax.broadcasted_iota(jnp.int32, (C, C), 0) + lax.broadcasted_iota(jnp.int32, (C, C), 1) == C - 1
    mirrored = jnp.dot(
        mirror.astype(jnp.float32), moved, precision=lax.Precision.HIGHEST, preferred_element_type=jnp.float32
    )
    pairs = []
    for pair in range(2):
        lanes = slice(pair * LANES, (pair + 1) * LANES)
        flip = pack(flips[2 * pair : 2 * pair + 1], flips[2 * pair + 1 : 2 * pair + 2])
        pairs.append(jnp.where(flip > 0, mirrored[:, lanes], moved[:, lanes]))
    pad_ref[0:C] = first_twin(pairs[0])
    pad_ref[CELLS + C : CELLS + 2 * C] = second_twin(pairs[0])
    west_ref[...] = first_twin(pairs[1])
    east_ref[...] = second_twin(pairs[1])


def row_of(i):
    return pl.ds(pl.multiple_of(i * C, C), C)


def lateral(pad_ref, west_ref, east_ref, i):
    own = pad_ref[row_of(i + 1)]
    column = lax.broadcasted_iota(jnp.int32, own.shape, 0)
    west = jnp.where(column == 0, west_ref[pl.ds(i, 1)], pltpu.roll(own, 1, 0))
    east = jnp.where(column == C - 1, east_ref[pl.ds(i, 1)], pltpu.roll(own, C - 1, 0))
    return own, (pad_ref[row_of(i)], pad_ref[row_of(i + 2)], west, east)


def coupled(conds, beside):
    total = conds[0] * beside[0]
    for cond, value in zip(conds[1:], beside[1:]):
        total = total + cond * value
    return total


def smooth_row(i, force, cond_total, own, image, residual_ref, smoothed_ref):
    cubic = cubic_weight * own * own
    residual = force - ((cond_total + cubic) * own - image)
    residual_ref[row_of(i)] = residual
    smoothed_ref[row_of(i)] = relax_factor * residual / (cond_total + 3.0 * cubic)


def pack_halves(smoothed_ref, packed_ref):
    packed_ref[...] = pack(smoothed_ref[: CELLS // 2], smoothed_ref[CELLS // 2 :])


def unpack_row(packed_ref, i, upper):
    block = packed_ref[row_of(i)]
    return second_twin(block) if upper else first_twin(block)


def unpack_halves(packed_ref, target_ref):
    target_ref[: CELLS // 2] = first_twin(packed_ref[...])
    target_ref[CELLS // 2 :] = second_twin(packed_ref[...])


def every(ref, start, count):
    return ref[pl.ds(start, count, stride=2)]


def rows_loop(count, step, body):
    @pl.loop(0, count, step=step)
    def _(first):
        for part in range(step):
            body(first + part)


def turned_layer(arrived_ref, first_field, second_field, group):
    parts = [arrived_ref[pl.ds(8 * field + group, TILES, stride=24)] for field in (first_field, second_field)]
    return jnp.concatenate(parts, axis=0).T


def spread_kernel(arrived_ref, pair_ref):
    for group in range(8):
        pair_ref[group * LANES : (group + 1) * LANES] = turned_layer(arrived_ref, 0, 1, group)


def lateral_kernel(
    arrived_ref, pair_ref, gluing_ref, flips_ref, viscous_ref, velocity_ref, force_ref, conds_ref, image_ref,
    total_ref, faces_ref, viscous_pad, viscous_west, viscous_east, pad, west, east,
):
    gluing, flips = gluing_ref[...], flips_ref[...]
    viscous_ref[...] = first_twin(pair_ref[...])
    velocity_ref[...] = second_twin(pair_ref[...])
    viscous_pad[C : C + CELLS] = viscous_ref[...]
    pad[C : C + CELLS] = velocity_ref[...]
    fine_ghosts(viscous_pad, viscous_west, viscous_east, gluing, flips)
    fine_ghosts(pad, west, east, gluing, flips)

    def body(i):
        own, beside = lateral(viscous_pad, viscous_west, viscous_east, i)
        conds = [0.5 * (own + other) for other in beside]
        for direction in range(4):
            conds_ref[direction, row_of(i)] = conds[direction]
        image_ref[row_of(i)] = coupled(conds, lateral(pad, west, east, i)[1])
        total_ref[row_of(i)] = conds[0] + conds[1] + conds[2] + conds[3]

    rows_loop(C, 4, body)
    sums, wests = [], []
    for big in range(HALF):
        upper, lower = big * 2 * C, big * 2 * C + C
        cells = slice(big * HALF, (big + 1) * HALF)

        def both(ref, start):
            return every(ref, start, HALF) + every(ref, start + 1, HALF)

        def column(direction, start):
            ref = conds_ref.at[direction]
            return every(ref, upper + start, HALF) + every(ref, lower + start, HALF)

        faces = pack(both(conds_ref.at[1], lower), column(3, 1))
        faces_ref[cells] = faces
        if big == 0:
            north = both(conds_ref.at[0], upper)
        wests.append(column(2, 0)[0:1])
        sums.append(both(viscous_ref, upper) + both(viscous_ref, lower))
    start = COARSE + COARSE // 2
    edge = pack(north, jnp.concatenate(wests, axis=0))
    for big in range(HALF // 2):
        first = COARSE + big * HALF
        faces_ref[first : first + HALF] = pack(sums[big], sums[big + HALF // 2])
    faces_ref[start : start + HALF] = edge
    for group in range(8):
        force_ref[group * LANES : (group + 1) * LANES] = turned_layer(arrived_ref, 2, 2, group)


def first_kernel(
    force_ref, viscous_ref, velocity_ref, lateral_ref, lateral_total_ref, above_ref, below_ref,
    radials_ref, total_ref, residual_ref, smoothed_ref, packed_ref,
):
    def body(i):
        here = row_of(i)
        viscous, velocity = viscous_ref[here], velocity_ref[here]
        beside = above_ref[here], below_ref[here]
        conds = [radial_weight * 0.5 * (viscous + first_twin(pair)) for pair in beside]
        cond_total = lateral_total_ref[here] + conds[0] + conds[1]
        radials_ref[0, here] = conds[0]
        radials_ref[1, here] = conds[1]
        total_ref[here] = cond_total
        image = lateral_ref[here] + conds[0] * second_twin(beside[0]) + conds[1] * second_twin(beside[1])
        smooth_row(i, force_ref[here], cond_total, velocity, image, residual_ref, smoothed_ref)

    rows_loop(C, 4, body)
    pack_halves(smoothed_ref, packed_ref)


def remain_kernel(
    conds_ref, radials_ref, total_ref, velocity_ref, residual_ref, smoothed_ref, above_ref, below_ref,
    gluing_ref, flips_ref, *rest,
):
    *faces, coarse_ref, pad, west, east, remain, damping = rest
    for faces_ref in faces:
        for copy in range(CHIPS):
            coarse_ref[copy, COARSE:] = faces_ref[...]
    pad[C : C + CELLS] = smoothed_ref[...]
    fine_ghosts(pad, west, east, gluing_ref[...], flips_ref[...])
    for upper in range(2):
        offset = upper * (C // 2)

        def body(source, upper=upper, offset=offset):
            i = source + offset
            here = row_of(i)
            velocity = velocity_ref[here]
            damp = 3.0 * (cubic_weight * velocity * velocity)
            own, beside = lateral(pad, west, east, i)
            beside = beside + (unpack_row(above_ref, source, upper), unpack_row(below_ref, source, upper))
            conds = [conds_ref[direction, here] for direction in range(4)]
            conds += [radials_ref[direction, here] for direction in range(2)]
            image = (total_ref[here] + damp) * own - coupled(conds, beside)
            remain[here] = residual_ref[here] - image
            damping[here] = damp

        rows_loop(C // 2, 4, body)

    for big in range(HALF):
        sums = []
        for ref in (remain, damping):
            start = big * 2 * C
            sums.append(
                every(ref, start, HALF)
                + every(ref, start + 1, HALF)
                + every(ref, start + C, HALF)
                + every(ref, start + C + 1, HALF)
            )
        cells = slice(big * HALF, (big + 1) * HALF)
        sums = pack(sums[0], sums[1])
        for copy in range(CHIPS):
            coarse_ref[copy, cells] = sums


def for_core(place_ref, own_ref, other_ref, body):
    @pl.when(place_ref[0] % 2 == 0)
    def _():
        body(own_ref, other_ref)

    @pl.when(place_ref[0] % 2 == 1)
    def _():
        body(other_ref, own_ref)


def radial_pair(values):
    swapped = swap(values)
    shaped = swapped.reshape(values.shape[0] // 8, 8, LANES)
    before = pltpu.roll(shaped, 1, 1).reshape(values.shape)
    after = pltpu.roll(shaped, 7, 1).reshape(values.shape)
    return pack(swapped, after), pack(before, swapped)


def faces_kernel(
    place_ref, own_ref, other_ref, rows_ref, columns_ref, up_ref, down_ref, face_total_ref, sums
):
    first, middle, last = COARSE, 2 * COARSE, 2 * COARSE + COARSE // 2
    half = COARSE // 2

    def arrange(even_ref, odd_ref):
        for sub in range(8):
            a, b = even_ref[sub, first:middle], odd_ref[sub, first:middle]
            rows_ref[pl.ds(LANES + sub, COARSE, stride=8)] = pack(a, swap(b))
            east = pack(swap(a), b)
            for big in range(HALF):
                columns_ref[big, pl.ds(8 + sub, HALF, stride=8)] = east[big * HALF : (big + 1) * HALF]
            a, b = even_ref[sub, middle:last], odd_ref[sub, middle:last]
            sums[pl.ds(sub, half, stride=8)] = pack(a, swap(b))
            sums[pl.ds(8 * half + sub, half, stride=8)] = pack(swap(a), b)
            a, b = even_ref[sub, last : last + HALF], odd_ref[sub, last : last + HALF]
            rows_ref[pl.ds(sub, HALF, stride=8)] = pack(a, swap(b))
            west = pack(swap(a), b)
            for big in range(HALF):
                columns_ref[big, sub : sub + 1] = west[big : big + 1]

    for_core(place_ref, own_ref, other_ref, arrange)
    side = HALF * 8
    shape = (side, LANES)
    row = lax.broadcasted_iota(jnp.int32, shape, 0) % 8
    lane = lax.broadcasted_iota(jnp.int32, shape, 1)
    top = (row == 7) & (lane >= TILES)
    bottom = (row == 0) & (lane < TILES)

    @pl.loop(0, HALF)
    def _(big):
        here = pl.ds(pl.multiple_of(big * side, side), side)
        own = sums[here]
        above, below = radial_pair(own)
        up = radial_weight * 0.5 * (own + jnp.where(top, 0.0, above))
        down = radial_weight * 0.5 * (own + jnp.where(bottom, 0.0, below))
        up_ref[here] = jnp.where(top, 0.0, up)
        down_ref[here] = jnp.where(bottom, 0.0, down)
        face_total_ref[here] = (
            rows_ref[here]
            + rows_ref[pl.ds(pl.multiple_of((big + 1) * side, side), side)]
            + columns_ref[big, :side]
            + columns_ref[big, 8 : 8 + side]
            + up
            + down
        )


def coarse_ghosts(pad, gluing, flips):
    side = HALF * 8
    inner = slice(8, 8 + side)
    north, south = pad[1, inner], pad[HALF, inner]
    west = pad[1 : HALF + 1, 8:16].reshape(side, LANES)
    east = pad[1 : HALF + 1, side : side + 8].reshape(side, LANES)
    first = jnp.concatenate([pack(north, swap(south)), pack(west, swap(east))], axis=1)
    second = jnp.concatenate([pack(swap(north), south), pack(swap(west), east)], axis=1)
    moved = glued(jnp.concatenate([first, second], axis=0), gluing)
    ghosts = []
    for pair in range(2):
        lanes = slice(pair * LANES, (pair + 1) * LANES)
        a, b = moved[:side, lanes], moved[side:, lanes]
        ghosts += [pack(a, swap(b)), pack(swap(a), b)]
    for number, ghost in enumerate(ghosts):
        flip = jnp.broadcast_to(flips[number : number + 1], (8, LANES)) > 0
        for k in range(HALF):
            other = HALF - 1 - k
            value = jnp.where(flip, ghost[8 * other : 8 * other + 8], ghost[8 * k : 8 * k + 8])
            if number < 2:
                pad[0 if number == 0 else HALF + 1, 8 + 8 * k : 16 + 8 * k] = value
            else:
                column = 0 if number == 2 else 8 + side
                pad[1 + k, column : column + 8] = value


def total_of(x):
    return jnp.sum(jnp.sum(x, axis=0, keepdims=True), axis=1, keepdims=True)


def folded(x):
    return jnp.sum(x.reshape(x.shape[0] // 8, 8, LANES), axis=0)


def solve_coarse(
    place_ref, own_ref, other_ref, rows_ref, columns_ref, up_ref, down_ref, face_total_ref, gluing, flips,
    pad, diagonal, image, residual, solution,
):
    side = HALF * 8
    inner = slice(8, 8 + side)
    chunk = 64

    def arrange(even_ref, odd_ref):
        for sub in range(8):
            a, b = even_ref[sub, :COARSE], odd_ref[sub, :COARSE]
            residual[pl.ds(sub, COARSE, stride=8)] = pack(a, swap(b))
            diagonal[pl.ds(sub, COARSE, stride=8)] = pack(swap(a), b)

    for_core(place_ref, own_ref, other_ref, arrange)
    zero = jnp.zeros((8, LANES), jnp.float32)

    def here_of(big):
        return pl.ds(pl.multiple_of(big * side, side), side)

    def total_over(body):
        def several(first, total):
            for part in range(4):
                total = body(first * 4 + part, total)
            return total

        return total_of(lax.fori_loop(0, HALF // 4, several, zero))

    def start(big, total):
        here = here_of(big)
        values = residual[here]
        pad[big + 1, inner] = values
        diagonal[here] = diagonal[here] + face_total_ref[here]
        return total + folded(values * values)

    norm = total_over(start)

    def apply_row(big, total):
        for part in range(side // chunk):
            first = part * chunk
            here = pl.ds(pl.multiple_of(big * side + first, chunk), chunk)
            own = pad[big + 1, 8 + first : 8 + first + chunk]
            above, below = radial_pair(own)
            south = pl.ds(pl.multiple_of((big + 1) * side + first, chunk), chunk)
            value = (
                rows_ref[here] * pad[big, 8 + first : 8 + first + chunk]
                + rows_ref[south] * pad[big + 2, 8 + first : 8 + first + chunk]
                + columns_ref[big, first : first + chunk] * pad[big + 1, first : first + chunk]
                + columns_ref[big, 8 + first : 8 + first + chunk] * pad[big + 1, 16 + first : 16 + first + chunk]
                + up_ref[here] * above
                + down_ref[here] * below
            )
            value = diagonal[here] * own - value
            image[here] = value
            total = total + folded(own * value)
        return total

    for step in range(CG_ITERS):
        coarse_ghosts(pad, gluing, flips)
        length = norm / total_over(apply_row)

        def advance(big, total, length=length, step=step):
            here = here_of(big)
            moved = length * pad[big + 1, inner]
            solution[here] = moved if step == 0 else solution[here] + moved
            if step + 1 == CG_ITERS:
                return total
            values = residual[here] - length * image[here]
            residual[here] = values
            return total + folded(values * values)

        following = total_over(advance)
        if step + 1 < CG_ITERS:
            ratio = following / norm
            norm = following

            def turn(big, total, ratio=ratio):
                pad[big + 1, inner] = residual[here_of(big)] + ratio * pad[big + 1, inner]
                return total

            total_over(turn)


def prolong_layer(solution, layer, target):
    inside = (layer >= 0) & (layer < NR)
    place = jnp.clip(layer, 0, NR - 1)
    values = solution[pl.ds(place // 2, COARSE, stride=8)]
    values = jnp.where(place % 2 == 0, first_twin(values), second_twin(values))
    values = jnp.where(inside, values, 0.0)
    for big in range(HALF):
        row = values[big * HALF : (big + 1) * HALF]
        for start in (0, 1, C, C + 1):
            target[pl.ds(big * 2 * C + start, HALF, stride=2)] = row


COARSE_SCRATCH = [
    pltpu.VMEM((HALF + 2, (HALF + 2) * 8, LANES), jnp.float32),
    *[pltpu.VMEM((COARSE * 8, LANES), jnp.float32) for _ in range(4)],
]


def step_kernel(
    place_ref, own_ref, other_ref, rows_ref, columns_ref, up_ref, down_ref, face_total_ref, gluing_ref, flips_ref,
    velocity_ref, above_ref, below_ref, smoothed_ref, smoothed_above_ref, smoothed_below_ref, force_ref,
    conds_ref, radials_ref, total_ref, new_velocity_ref, new_residual_ref, new_smoothed_ref, packed_ref,
    pad, diagonal, image, residual, solution, velocity, west, east, above, below, spread,
):
    gluing, flips = gluing_ref[...], flips_ref[...]
    for pairs, smooth, target in ((above_ref, smoothed_above_ref, above), (below_ref, smoothed_below_ref, below)):
        unpack_halves(smooth, target)
        target[...] = target[...] + second_twin(pairs[...])
    solve_coarse(
        place_ref, own_ref, other_ref, rows_ref, columns_ref, up_ref, down_ref, face_total_ref, gluing, flips,
        pad, diagonal, image, residual, solution,
    )
    layer = place_ref[0]
    prolong_layer(solution, layer, spread)
    velocity[C : C + CELLS] = velocity_ref[...] + smoothed_ref[...] + spread[...]
    new_velocity_ref[...] = velocity[C : C + CELLS]
    fine_ghosts(velocity, west, east, gluing, flips)
    for shift, target in ((1, above), (-1, below)):
        prolong_layer(solution, layer + shift, spread)
        target[...] = target[...] + spread[...]

    def body(i):
        here = row_of(i)
        own, beside = lateral(velocity, west, east, i)
        beside = beside + (above[here], below[here])
        conds = [conds_ref[direction, here] for direction in range(4)]
        conds += [radials_ref[direction, here] for direction in range(2)]
        smooth_row(i, force_ref[here], total_ref[here], own, coupled(conds, beside), new_residual_ref, new_smoothed_ref)

    rows_loop(C, 4, body)
    pack_halves(new_smoothed_ref, packed_ref)


def last_kernel(
    place_ref, own_ref, other_ref, rows_ref, columns_ref, up_ref, down_ref, face_total_ref, gluing_ref, flips_ref,
    velocity_ref, smoothed_ref, out_ref, pad, diagonal, image, residual, solution, spread, turned,
):
    solve_coarse(
        place_ref, own_ref, other_ref, rows_ref, columns_ref, up_ref, down_ref, face_total_ref,
        gluing_ref[...], flips_ref[...], pad, diagonal, image, residual, solution,
    )
    prolong_layer(solution, place_ref[0], spread)
    for group in range(8):
        cells = slice(group * LANES, (group + 1) * LANES)
        turned[cells] = (velocity_ref[cells] + smoothed_ref[cells] + spread[cells]).T
    for group in range(8):
        out_ref[group : group + 1] = turned[pl.ds(group * LANES + place_ref[1], 1)]


def call(kernel, outs, scratch, args, scalars=0, mebibytes=4):
    vmem = pl.BlockSpec(memory_space=pltpu.VMEM)
    shapes = [jax.ShapeDtypeStruct(shape, jnp.float32) for shape in outs]
    return pl.pallas_call(
        kernel,
        out_shape=shapes,
        in_specs=[pl.BlockSpec(memory_space=pltpu.SMEM)] * scalars + [vmem] * (len(args) - scalars),
        out_specs=[vmem] * len(outs),
        scratch_shapes=[pltpu.VMEM(shape, jnp.float32) for shape in scratch],
        compiler_params=pltpu.CompilerParams(vmem_limit_bytes=VMEM_MIB << 20),
        cost_estimate=pl.CostEstimate(flops=mebibytes << 20, bytes_accessed=mebibytes << 20, transcendentals=0),
    )(*args)


VMEM_MIB = 20
PADDED = (CELLS + 2 * C, LANES)
FINE = (CELLS, LANES)
PACKED = (CELLS // 2, LANES)
EDGE = (C, LANES)
FACES = (COARSE + COARSE // 2 + HALF, LANES)
GRID = (COARSE * 8, LANES)
COARSE_SCRATCH = [(HALF + 2, (HALF + 2) * 8, LANES)] + [GRID] * 4


def spread_layer(arrived):
    return call(spread_kernel, [FINE], [], [arrived])[0]


def lateral_stage(*args):
    outs = [FINE, FINE, FINE, (4,) + FINE, FINE, FINE, FACES]
    return call(lateral_kernel, outs, [PADDED, EDGE, EDGE, PADDED, EDGE, EDGE], args, mebibytes=24)


def first_stage(*args):
    return call(first_kernel, [(2,) + FINE, FINE, FINE, FINE, PACKED], [], args)


def remain_stage(*args, faces=None):
    rows = COARSE
    if faces is not None:
        args, rows = args + (faces,), COARSE + FACES[0]
    return call(remain_kernel, [(CHIPS, rows, LANES)], [PADDED, EDGE, EDGE, FINE, FINE], args)[0]


def faces_stage(*args):
    outs = [((HALF + 1) * HALF * 8, LANES), (HALF, (HALF + 1) * 8, LANES)] + [GRID] * 3
    return call(faces_kernel, outs, [GRID], args, 1, 24)


def step_stage(*args):
    scratch = COARSE_SCRATCH + [PADDED, EDGE, EDGE, FINE, FINE, FINE]
    return call(step_kernel, [FINE, FINE, FINE, PACKED], scratch, args, 1)


def last_stage(*args):
    return call(last_kernel, [(8, LANES)], COARSE_SCRATCH + [FINE, FINE], args, 1)[0]


NEAR = 4
FAR = TILES // NEAR


def place_of(tile):
    return tile // 2 % NEAR * FAR + tile // (2 * NEAR) * 2 + tile % 2


def gluing_tables(glue_tile, glue_side, glue_flip):
    def lanes_of(table):
        return table.reshape(FAR // 2, NEAR, 2, 4).transpose(3, 1, 0, 2).reshape(4, TILES)

    source = (lanes_of(glue_side) * TILES + place_of(lanes_of(glue_tile))).reshape(1, 4 * TILES)
    gluing = (jnp.arange(4 * TILES)[:, None] == source).astype(jnp.bfloat16)
    flips = lanes_of(glue_flip).astype(jnp.float32)
    flips = jnp.concatenate([flips, flips], axis=1)
    return gluing, jnp.concatenate([flips, flips], axis=0)


def gather(values, axis, groups):
    sent = jnp.broadcast_to(values[None], (len(groups[0]),) + values.shape)
    arrived = lax.all_to_all(sent, axis, split_axis=0, concat_axis=0, axis_index_groups=groups, tiled=True)
    return arrived.reshape((-1,) + values.shape[1:])


def gather_lateral(values):
    tiles = sorted(range(TILES), key=place_of)
    far = [tiles[near * FAR : (near + 1) * FAR] for near in range(NEAR)]
    return gather(gather(values, "lat", far), "lat", [list(group) for group in zip(*far)])


def gather_cores(copies):
    groups = [list(range(core, NR, 2)) for core in range(2)]
    return lax.all_to_all(copies, "rad", split_axis=0, concat_axis=0, axis_index_groups=groups, tiled=True)


def swap_cores(own):
    return lax.ppermute(own, "rad", [(layer, layer ^ 1) for layer in range(NR)])


def gather_radial(copies):
    own = gather_cores(copies)
    return own, swap_cores(own)


def radial(values):
    lat = lax.axis_size("lat")
    above, below = [], []
    for tile in range(lat):
        for layer in range(NR - 1):
            other = tile ^ 1 if layer % 4 == 3 else tile
            above.append((other * NR + layer + 1, tile * NR + layer))
            below.append((tile * NR + layer, other * NR + layer + 1))
    return lax.ppermute(values, ("lat", "rad"), above), lax.ppermute(values, ("lat", "rad"), below)


def on_device(rhs_force, viscosity, initial_guess, glue_tile, glue_side, glue_flip):
    tables = gluing_tables(glue_tile, glue_side, glue_flip)
    place = jnp.stack([lax.axis_index("rad"), place_of(lax.axis_index("lat"))]).astype(jnp.int32)
    own = jnp.concatenate([field.reshape(8, LANES) for field in (viscosity, initial_guess, rhs_force)], axis=0)
    own, place = lax.optimization_barrier((own, place))
    arrived = gather_lateral(own)
    pair = spread_layer(arrived)
    pair_beside = radial(pair)
    viscous, velocity, force, conds, lateral_image, lateral_total, faces = lateral_stage(arrived, pair, *tables)
    radials, total, residual, smoothed, packed = first_stage(
        force, viscous, velocity, lateral_image, lateral_total, *pair_beside
    )
    smoothed_beside = radial(packed)
    coarse = remain_stage(
        conds, radials, total, velocity, residual, smoothed, *smoothed_beside, *tables, faces=faces
    )
    coarse = gather_radial(coarse)
    coefficients = faces_stage(place, *coarse)
    velocity, residual, smoothed, packed = step_stage(
        place, *coarse, *coefficients, *tables, velocity, *pair_beside, smoothed,
        *smoothed_beside, force, conds, radials, total,
    )
    smoothed_beside = radial(packed)
    coarse = remain_stage(conds, radials, total, velocity, residual, smoothed, *smoothed_beside, *tables)
    out = last_stage(place, *gather_radial(coarse), *coefficients, *tables, velocity, smoothed)
    return out.reshape(1, CELLS)


def solution(mesh):
    return jax.shard_map(
        on_device,
        mesh=mesh,
        in_specs=(P("rad", "lat"), P("rad", "lat"), P("rad", "lat"), P(), P(), P()),
        out_specs=P("rad", "lat"),
        check_vma=False,
    )
```

```python
import functools

import jax
import jax.numpy as jnp
from jax import lax
from jax.experimental import pallas as pl
from jax.experimental.pallas import tpu as pltpu
from jax.sharding import PartitionSpec as P

C = 32
HALF = 16
TILES = 64
NR = 16
CHIPS = NR // 2
CELLS = C * C
COARSE = HALF * HALF
LANES = 128
CG_ITERS = 4

cubic_weight = 8.0
radial_weight = 4.0
relax_factor = 0.8


def low(x):
    return lax.broadcasted_iota(jnp.int32, x.shape, x.ndim - 1) < TILES


def swap(x):
    return pltpu.roll(x, TILES, x.ndim - 1)


def pack(a, b):
    return jnp.where(low(a), a, b)


def first_twin(x):
    return jnp.where(low(x), x, swap(x))


def second_twin(x):
    return jnp.where(low(x), swap(x), x)


def glued(values, gluing):
    rows = values.shape[0]
    high = values.astype(jnp.bfloat16)
    rest = values - high.astype(jnp.float32)
    middle = rest.astype(jnp.bfloat16)
    lowest = (rest - middle.astype(jnp.float32)).astype(jnp.bfloat16)
    moved = jnp.dot(
        jnp.concatenate([high, middle, lowest], axis=0), gluing, preferred_element_type=jnp.float32
    )
    return moved[:rows] + (moved[rows : 2 * rows] + moved[2 * rows :])


def fine_ghosts(pad_ref, west_ref, east_ref, gluing, flips):
    north, south = pad_ref[C : 2 * C], pad_ref[CELLS : CELLS + C]
    west, east = pad_ref[pl.ds(C, C, stride=C)], pad_ref[pl.ds(2 * C - 1, C, stride=C)]
    moved = glued(jnp.concatenate([pack(north, south), pack(west, east)], axis=1), gluing)
    mirror = lax.broadcasted_iota(jnp.int32, (C, C), 0) + lax.broadcasted_iota(jnp.int32, (C, C), 1) == C - 1
    mirrored = jnp.dot(
        mirror.astype(jnp.float32), moved, precision=lax.Precision.HIGHEST, preferred_element_type=jnp.float32
    )
    pairs = []
    for pair in range(2):
        lanes = slice(pair * LANES, (pair + 1) * LANES)
        flip = pack(flips[2 * pair : 2 * pair + 1], flips[2 * pair + 1 : 2 * pair + 2])
        pairs.append(jnp.where(flip > 0, mirrored[:, lanes], moved[:, lanes]))
    pad_ref[0:C] = first_twin(pairs[0])
    pad_ref[CELLS + C : CELLS + 2 * C] = second_twin(pairs[0])
    west_ref[...] = first_twin(pairs[1])
    east_ref[...] = second_twin(pairs[1])


def row_of(i):
    return pl.ds(pl.multiple_of(i * C, C), C)


def lateral(pad_ref, west_ref, east_ref, i):
    own = pad_ref[row_of(i + 1)]
    column = lax.broadcasted_iota(jnp.int32, own.shape, 0)
    west = jnp.where(column == 0, west_ref[pl.ds(i, 1)], pltpu.roll(own, 1, 0))
    east = jnp.where(column == C - 1, east_ref[pl.ds(i, 1)], pltpu.roll(own, C - 1, 0))
    return own, (pad_ref[row_of(i)], pad_ref[row_of(i + 2)], west, east)


def coupled(conds, beside):
    total = conds[0] * beside[0]
    for cond, value in zip(conds[1:], beside[1:]):
        total = total + cond * value
    return total


def smooth_row(i, force, cond_total, own, image, residual_ref, smoothed_ref):
    cubic = cubic_weight * own * own
    residual = force - ((cond_total + cubic) * own - image)
    residual_ref[row_of(i)] = residual
    smoothed_ref[row_of(i)] = relax_factor * residual / (cond_total + 3.0 * cubic)


def pack_halves(smoothed_ref, packed_ref):
    packed_ref[...] = pack(smoothed_ref[: CELLS // 2], smoothed_ref[CELLS // 2 :])


def unpack_row(packed_ref, i, upper):
    block = packed_ref[row_of(i)]
    return second_twin(block) if upper else first_twin(block)


def unpack_halves(packed_ref, target_ref):
    target_ref[: CELLS // 2] = first_twin(packed_ref[...])
    target_ref[CELLS // 2 :] = second_twin(packed_ref[...])


def every(ref, start, count):
    return ref[pl.ds(start, count, stride=2)]


def rows_loop(count, step, body):
    @pl.loop(0, count, step=step)
    def _(first):
        for part in range(step):
            body(first + part)


def turned_layer(arrived_ref, first_field, second_field, group):
    parts = [arrived_ref[pl.ds(8 * field + group, TILES, stride=24)] for field in (first_field, second_field)]
    return jnp.concatenate(parts, axis=0).T


def spread_kernel(arrived_ref, pair_ref):
    for group in range(8):
        pair_ref[group * LANES : (group + 1) * LANES] = turned_layer(arrived_ref, 0, 1, group)


def lateral_kernel(
    arrived_ref, pair_ref, gluing_ref, flips_ref, viscous_ref, velocity_ref, force_ref, conds_ref, image_ref,
    total_ref, faces_ref, viscous_pad, viscous_west, viscous_east, pad, west, east,
):
    gluing, flips = gluing_ref[...], flips_ref[...]
    viscous_ref[...] = first_twin(pair_ref[...])
    velocity_ref[...] = second_twin(pair_ref[...])
    viscous_pad[C : C + CELLS] = viscous_ref[...]
    pad[C : C + CELLS] = velocity_ref[...]
    fine_ghosts(viscous_pad, viscous_west, viscous_east, gluing, flips)
    fine_ghosts(pad, west, east, gluing, flips)

    def body(i):
        own, beside = lateral(viscous_pad, viscous_west, viscous_east, i)
        conds = [0.5 * (own + other) for other in beside]
        for direction in range(4):
            conds_ref[direction, row_of(i)] = conds[direction]
        image_ref[row_of(i)] = coupled(conds, lateral(pad, west, east, i)[1])
        total_ref[row_of(i)] = conds[0] + conds[1] + conds[2] + conds[3]

    rows_loop(C, 4, body)
    sums, wests = [], []
    for big in range(HALF):
        upper, lower = big * 2 * C, big * 2 * C + C
        cells = slice(big * HALF, (big + 1) * HALF)

        def both(ref, start):
            return every(ref, start, HALF) + every(ref, start + 1, HALF)

        def column(direction, start):
            ref = conds_ref.at[direction]
            return every(ref, upper + start, HALF) + every(ref, lower + start, HALF)

        faces = pack(both(conds_ref.at[1], lower), column(3, 1))
        faces_ref[cells] = faces
        if big == 0:
            north = both(conds_ref.at[0], upper)
        wests.append(column(2, 0)[0:1])
        sums.append(both(viscous_ref, upper) + both(viscous_ref, lower))
    start = COARSE + COARSE // 2
    edge = pack(north, jnp.concatenate(wests, axis=0))
    for big in range(HALF // 2):
        first = COARSE + big * HALF
        faces_ref[first : first + HALF] = pack(sums[big], sums[big + HALF // 2])
    faces_ref[start : start + HALF] = edge
    for group in range(8):
        force_ref[group * LANES : (group + 1) * LANES] = turned_layer(arrived_ref, 2, 2, group)


def first_kernel(
    force_ref, viscous_ref, velocity_ref, lateral_ref, lateral_total_ref, above_ref, below_ref,
    radials_ref, total_ref, residual_ref, smoothed_ref, packed_ref,
):
    def body(i):
        here = row_of(i)
        viscous, velocity = viscous_ref[here], velocity_ref[here]
        beside = above_ref[here], below_ref[here]
        conds = [radial_weight * 0.5 * (viscous + first_twin(pair)) for pair in beside]
        cond_total = lateral_total_ref[here] + conds[0] + conds[1]
        radials_ref[0, here] = conds[0]
        radials_ref[1, here] = conds[1]
        total_ref[here] = cond_total
        image = lateral_ref[here] + conds[0] * second_twin(beside[0]) + conds[1] * second_twin(beside[1])
        smooth_row(i, force_ref[here], cond_total, velocity, image, residual_ref, smoothed_ref)

    rows_loop(C, 4, body)
    pack_halves(smoothed_ref, packed_ref)


def remain_kernel(
    conds_ref, radials_ref, total_ref, velocity_ref, residual_ref, smoothed_ref, above_ref, below_ref,
    gluing_ref, flips_ref, *rest,
):
    *faces, coarse_ref, pad, west, east, remain, damping = rest
    for faces_ref in faces:
        for copy in range(CHIPS):
            coarse_ref[copy, COARSE:] = faces_ref[...]
    pad[C : C + CELLS] = smoothed_ref[...]
    fine_ghosts(pad, west, east, gluing_ref[...], flips_ref[...])
    for upper in range(2):
        offset = upper * (C // 2)

        def body(source, upper=upper, offset=offset):
            i = source + offset
            here = row_of(i)
            velocity = velocity_ref[here]
            damp = 3.0 * (cubic_weight * velocity * velocity)
            own, beside = lateral(pad, west, east, i)
            beside = beside + (unpack_row(above_ref, source, upper), unpack_row(below_ref, source, upper))
            conds = [conds_ref[direction, here] for direction in range(4)]
            conds += [radials_ref[direction, here] for direction in range(2)]
            image = (total_ref[here] + damp) * own - coupled(conds, beside)
            remain[here] = residual_ref[here] - image
            damping[here] = damp

        rows_loop(C // 2, 4, body)

    for big in range(HALF):
        sums = []
        for ref in (remain, damping):
            start = big * 2 * C
            sums.append(
                every(ref, start, HALF)
                + every(ref, start + 1, HALF)
                + every(ref, start + C, HALF)
                + every(ref, start + C + 1, HALF)
            )
        cells = slice(big * HALF, (big + 1) * HALF)
        sums = pack(sums[0], sums[1])
        for copy in range(CHIPS):
            coarse_ref[copy, cells] = sums


def for_core(place_ref, own_ref, other_ref, body):
    @pl.when(place_ref[0] % 2 == 0)
    def _():
        body(own_ref, other_ref)

    @pl.when(place_ref[0] % 2 == 1)
    def _():
        body(other_ref, own_ref)


def aligned(start, count):
    return pl.ds(pl.multiple_of(start, count), count)


def radial_pair(values):
    swapped = swap(values)
    shaped = swapped.reshape(values.shape[0] // 8, 8, LANES)
    before = pltpu.roll(shaped, 1, 1).reshape(values.shape)
    after = pltpu.roll(shaped, 7, 1).reshape(values.shape)
    return pack(swapped, after), pack(before, swapped)


def faces_kernel(
    place_ref, own_ref, other_ref, rows_ref, columns_ref, up_ref, down_ref, face_total_ref, sums
):
    first, middle, last = COARSE, 2 * COARSE, 2 * COARSE + COARSE // 2
    half = COARSE // 2

    def arrange(even_ref, odd_ref):
        for sub in range(8):
            a, b = even_ref[sub, first:middle], odd_ref[sub, first:middle]
            rows_ref[pl.ds(LANES + sub, COARSE, stride=8)] = pack(a, swap(b))
            east = pack(swap(a), b)
            for big in range(HALF):
                columns_ref[big, pl.ds(8 + sub, HALF, stride=8)] = east[big * HALF : (big + 1) * HALF]
            a, b = even_ref[sub, middle:last], odd_ref[sub, middle:last]
            sums[pl.ds(sub, half, stride=8)] = pack(a, swap(b))
            sums[pl.ds(8 * half + sub, half, stride=8)] = pack(swap(a), b)
            a, b = even_ref[sub, last : last + HALF], odd_ref[sub, last : last + HALF]
            rows_ref[pl.ds(sub, HALF, stride=8)] = pack(a, swap(b))
            west = pack(swap(a), b)
            for big in range(HALF):
                columns_ref[big, sub : sub + 1] = west[big : big + 1]

    for_core(place_ref, own_ref, other_ref, arrange)
    side = HALF * 8
    shape = (side, LANES)
    row = lax.broadcasted_iota(jnp.int32, shape, 0) % 8
    lane = lax.broadcasted_iota(jnp.int32, shape, 1)
    top = (row == 7) & (lane >= TILES)
    bottom = (row == 0) & (lane < TILES)

    @pl.loop(0, HALF)
    def _(big):
        here = pl.ds(pl.multiple_of(big * side, side), side)
        own = sums[here]
        above, below = radial_pair(own)
        up = radial_weight * 0.5 * (own + jnp.where(top, 0.0, above))
        down = radial_weight * 0.5 * (own + jnp.where(bottom, 0.0, below))
        up_ref[here] = jnp.where(top, 0.0, up)
        down_ref[here] = jnp.where(bottom, 0.0, down)
        face_total_ref[here] = (
            rows_ref[here]
            + rows_ref[pl.ds(pl.multiple_of((big + 1) * side, side), side)]
            + columns_ref[big, :side]
            + columns_ref[big, 8 : 8 + side]
            + up
            + down
        )


def coarse_ghosts(pad, gluing, flips):
    side = HALF * 8
    inner = slice(8, 8 + side)
    north, south = pad[1, inner], pad[HALF, inner]
    west = pad[1 : HALF + 1, 8:16].reshape(side, LANES)
    east = pad[1 : HALF + 1, side : side + 8].reshape(side, LANES)
    first = jnp.concatenate([pack(north, swap(south)), pack(west, swap(east))], axis=1)
    second = jnp.concatenate([pack(swap(north), south), pack(swap(west), east)], axis=1)
    moved = glued(jnp.concatenate([first, second], axis=0), gluing)
    ghosts = []
    for pair in range(2):
        lanes = slice(pair * LANES, (pair + 1) * LANES)
        a, b = moved[:side, lanes], moved[side:, lanes]
        ghosts += [pack(a, swap(b)), pack(swap(a), b)]
    for number, ghost in enumerate(ghosts):
        flip = jnp.broadcast_to(flips[number : number + 1], (8, LANES)) > 0
        for k in range(HALF):
            other = HALF - 1 - k
            value = jnp.where(flip, ghost[8 * other : 8 * other + 8], ghost[8 * k : 8 * k + 8])
            if number < 2:
                pad[0 if number == 0 else HALF + 1, 8 + 8 * k : 16 + 8 * k] = value
            else:
                column = 0 if number == 2 else 8 + side
                pad[1 + k, column : column + 8] = value


def total_of(x):
    return jnp.sum(jnp.sum(x, axis=0, keepdims=True), axis=1, keepdims=True)


def folded(x):
    return jnp.sum(x.reshape(x.shape[0] // 8, 8, LANES), axis=0)


def solve_coarse(
    place_ref, own_ref, other_ref, rows_ref, columns_ref, up_ref, down_ref, face_total_ref, gluing, flips,
    pad, diagonal, image, residual, solution,
):
    side = HALF * 8
    inner = slice(8, 8 + side)
    chunk = 64

    def arrange(even_ref, odd_ref):
        for sub in range(8):
            a, b = even_ref[sub, :COARSE], odd_ref[sub, :COARSE]
            residual[pl.ds(sub, COARSE, stride=8)] = pack(a, swap(b))
            diagonal[pl.ds(sub, COARSE, stride=8)] = pack(swap(a), b)

    for_core(place_ref, own_ref, other_ref, arrange)
    zero = jnp.zeros((8, LANES), jnp.float32)

    def here_of(big):
        return pl.ds(pl.multiple_of(big * side, side), side)

    def total_over(body):
        def several(first, total):
            for part in range(4):
                total = body(first * 4 + part, total)
            return total

        return total_of(lax.fori_loop(0, HALF // 4, several, zero))

    def start(big, total):
        here = here_of(big)
        values = residual[here]
        pad[big + 1, inner] = values
        diagonal[here] = diagonal[here] + face_total_ref[here]
        return total + folded(values * values)

    norm = total_over(start)

    def apply_rows(block, total):
        first = block * 4
        for part in range(side // chunk):
            start = part * chunk
            inside = slice(8 + start, 8 + start + chunk)
            before, own = pad[first, inside], pad[first + 1, inside]
            north = rows_ref[aligned(first * side + start, chunk)]
            for big in range(4):
                here = aligned((first + big) * side + start, chunk)
                after = pad[first + big + 2, inside]
                south = rows_ref[aligned((first + big + 1) * side + start, chunk)]
                columns = columns_ref[first + big, start : start + chunk + 8]
                west_end = pad[first + big + 1, start : start + 8]
                east_end = pad[first + big + 1, start + chunk + 8 : start + chunk + 16]
                row = jnp.concatenate([west_end, own, east_end], axis=0)
                above, below = radial_pair(own)
                value = (
                    north * before
                    + south * after
                    + columns[:chunk] * row[:chunk]
                    + columns[8:] * row[16:]
                    + up_ref[here] * above
                    + down_ref[here] * below
                )
                value = diagonal[here] * own - value
                image[here] = value
                total = total + folded(own * value)
                before, own, north = own, after, south
        return total

    for step in range(CG_ITERS):
        coarse_ghosts(pad, gluing, flips)
        length = norm / total_of(lax.fori_loop(0, HALF // 4, apply_rows, zero))

        def advance(big, total, length=length):
            here = here_of(big)
            values = residual[here] - length * image[here]
            residual[here] = values
            return total + folded(values * values)

        ratio = 0.0
        if step + 1 < CG_ITERS:
            following = total_over(advance)
            ratio = following / norm
            norm = following

        def turn(big, total, length=length, ratio=ratio, step=step):
            here = here_of(big)
            old = pad[big + 1, inner]
            solution[here] = length * old if step == 0 else solution[here] + length * old
            if step + 1 < CG_ITERS:
                pad[big + 1, inner] = residual[here] + ratio * old
            return total

        total_over(turn)


def prolong_layer(solution, layer, target):
    inside = (layer >= 0) & (layer < NR)
    place = jnp.clip(layer, 0, NR - 1)
    values = solution[pl.ds(place // 2, COARSE, stride=8)]
    values = jnp.where(place % 2 == 0, first_twin(values), second_twin(values))
    values = jnp.where(inside, values, 0.0)
    for big in range(HALF):
        row = values[big * HALF : (big + 1) * HALF]
        for start in (0, 1, C, C + 1):
            target[pl.ds(big * 2 * C + start, HALF, stride=2)] = row


COARSE_SCRATCH = [
    pltpu.VMEM((HALF + 2, (HALF + 2) * 8, LANES), jnp.float32),
    *[pltpu.VMEM((COARSE * 8, LANES), jnp.float32) for _ in range(4)],
]


def step_kernel(
    place_ref, own_ref, other_ref, rows_ref, columns_ref, up_ref, down_ref, face_total_ref, gluing_ref, flips_ref,
    velocity_ref, above_ref, below_ref, smoothed_ref, smoothed_above_ref, smoothed_below_ref, force_ref,
    conds_ref, radials_ref, total_ref, new_velocity_ref, new_residual_ref, new_smoothed_ref, packed_ref,
    pad, diagonal, image, residual, solution, velocity, west, east, above, below, spread,
):
    gluing, flips = gluing_ref[...], flips_ref[...]
    for pairs, smooth, target in ((above_ref, smoothed_above_ref, above), (below_ref, smoothed_below_ref, below)):
        unpack_halves(smooth, target)
        target[...] = target[...] + second_twin(pairs[...])
    solve_coarse(
        place_ref, own_ref, other_ref, rows_ref, columns_ref, up_ref, down_ref, face_total_ref, gluing, flips,
        pad, diagonal, image, residual, solution,
    )
    layer = place_ref[0]
    prolong_layer(solution, layer, spread)
    velocity[C : C + CELLS] = velocity_ref[...] + smoothed_ref[...] + spread[...]
    new_velocity_ref[...] = velocity[C : C + CELLS]
    fine_ghosts(velocity, west, east, gluing, flips)
    for shift, target in ((1, above), (-1, below)):
        prolong_layer(solution, layer + shift, spread)
        target[...] = target[...] + spread[...]

    def body(i):
        here = row_of(i)
        own, beside = lateral(velocity, west, east, i)
        beside = beside + (above[here], below[here])
        conds = [conds_ref[direction, here] for direction in range(4)]
        conds += [radials_ref[direction, here] for direction in range(2)]
        smooth_row(i, force_ref[here], total_ref[here], own, coupled(conds, beside), new_residual_ref, new_smoothed_ref)

    rows_loop(C, 4, body)
    pack_halves(new_smoothed_ref, packed_ref)


def last_kernel(
    place_ref, own_ref, other_ref, rows_ref, columns_ref, up_ref, down_ref, face_total_ref, gluing_ref, flips_ref,
    velocity_ref, smoothed_ref, out_ref, pad, diagonal, image, residual, solution, spread, turned,
):
    solve_coarse(
        place_ref, own_ref, other_ref, rows_ref, columns_ref, up_ref, down_ref, face_total_ref,
        gluing_ref[...], flips_ref[...], pad, diagonal, image, residual, solution,
    )
    prolong_layer(solution, place_ref[0], spread)
    for group in range(8):
        cells = slice(group * LANES, (group + 1) * LANES)
        turned[cells] = (velocity_ref[cells] + smoothed_ref[cells] + spread[cells]).T
    for group in range(8):
        out_ref[group : group + 1] = turned[pl.ds(group * LANES + place_ref[1], 1)]


def call(kernel, outs, scratch, args, scalars=0, mebibytes=4):
    vmem = pl.BlockSpec(memory_space=pltpu.VMEM)
    shapes = [jax.ShapeDtypeStruct(shape, jnp.float32) for shape in outs]
    return pl.pallas_call(
        kernel,
        out_shape=shapes,
        in_specs=[pl.BlockSpec(memory_space=pltpu.SMEM)] * scalars + [vmem] * (len(args) - scalars),
        out_specs=[vmem] * len(outs),
        scratch_shapes=[pltpu.VMEM(shape, jnp.float32) for shape in scratch],
        compiler_params=pltpu.CompilerParams(vmem_limit_bytes=VMEM_MIB << 20),
        cost_estimate=pl.CostEstimate(flops=mebibytes << 20, bytes_accessed=mebibytes << 20, transcendentals=0),
    )(*args)


VMEM_MIB = 20
PADDED = (CELLS + 2 * C, LANES)
FINE = (CELLS, LANES)
PACKED = (CELLS // 2, LANES)
EDGE = (C, LANES)
FACES = (COARSE + COARSE // 2 + HALF, LANES)
GRID = (COARSE * 8, LANES)
COARSE_SCRATCH = [(HALF + 2, (HALF + 2) * 8, LANES)] + [GRID] * 4


def spread_layer(arrived):
    return call(spread_kernel, [FINE], [], [arrived])[0]


def lateral_stage(*args):
    outs = [FINE, FINE, FINE, (4,) + FINE, FINE, FINE, FACES]
    return call(lateral_kernel, outs, [PADDED, EDGE, EDGE, PADDED, EDGE, EDGE], args, mebibytes=24)


def first_stage(*args):
    return call(first_kernel, [(2,) + FINE, FINE, FINE, FINE, PACKED], [], args)


def remain_stage(*args, faces=None):
    rows = COARSE
    if faces is not None:
        args, rows = args + (faces,), COARSE + FACES[0]
    return call(remain_kernel, [(CHIPS, rows, LANES)], [PADDED, EDGE, EDGE, FINE, FINE], args)[0]


def faces_stage(*args):
    outs = [((HALF + 1) * HALF * 8, LANES), (HALF, (HALF + 1) * 8, LANES)] + [GRID] * 3
    return call(faces_kernel, outs, [GRID], args, 1, 24)


def step_stage(*args):
    scratch = COARSE_SCRATCH + [PADDED, EDGE, EDGE, FINE, FINE, FINE]
    return call(step_kernel, [FINE, FINE, FINE, PACKED], scratch, args, 1)


def last_stage(*args):
    return call(last_kernel, [(8, LANES)], COARSE_SCRATCH + [FINE, FINE], args, 1)[0]


NEAR = 8
FAR = TILES // NEAR


def place_of(tile):
    return tile % NEAR * FAR + tile // NEAR


def gluing_tables(glue_tile, glue_side, glue_flip):
    def lanes_of(table):
        return table.reshape(FAR, NEAR, 4).transpose(2, 1, 0).reshape(4, TILES)

    source = (lanes_of(glue_side) * TILES + place_of(lanes_of(glue_tile))).reshape(1, 4 * TILES)
    gluing = (jnp.arange(4 * TILES)[:, None] == source).astype(jnp.bfloat16)
    flips = lanes_of(glue_flip).astype(jnp.float32)
    flips = jnp.concatenate([flips, flips], axis=1)
    return gluing, jnp.concatenate([flips, flips], axis=0)


def gather(values, axis, groups):
    sent = jnp.broadcast_to(values[None], (len(groups[0]),) + values.shape)
    arrived = lax.all_to_all(sent, axis, split_axis=0, concat_axis=0, axis_index_groups=groups, tiled=True)
    return arrived.reshape((-1,) + values.shape[1:])


def gather_lateral(values):
    tiles = sorted(range(TILES), key=place_of)
    far = [tiles[near * FAR : (near + 1) * FAR] for near in range(NEAR)]
    return gather(gather(values, "lat", far), "lat", [list(group) for group in zip(*far)])


def gather_cores(copies):
    groups = [list(range(core, NR, 2)) for core in range(2)]
    return lax.all_to_all(copies, "rad", split_axis=0, concat_axis=0, axis_index_groups=groups, tiled=True)


def swap_cores(own):
    return lax.ppermute(own, "rad", [(layer, layer ^ 1) for layer in range(NR)])


def gather_radial(copies):
    own = gather_cores(copies)
    return own, swap_cores(own)


def radial(values):
    lat = lax.axis_size("lat")
    above, below = [], []
    for tile in range(lat):
        for layer in range(NR - 1):
            other = tile ^ 1 if layer % 4 == 3 else tile
            above.append((other * NR + layer + 1, tile * NR + layer))
            below.append((tile * NR + layer, other * NR + layer + 1))
    return lax.ppermute(values, ("lat", "rad"), above), lax.ppermute(values, ("lat", "rad"), below)


def on_device(rhs_force, viscosity, initial_guess, glue_tile, glue_side, glue_flip):
    tables = gluing_tables(glue_tile, glue_side, glue_flip)
    place = jnp.stack([lax.axis_index("rad"), place_of(lax.axis_index("lat"))]).astype(jnp.int32)
    own = jnp.concatenate([field.reshape(8, LANES) for field in (viscosity, initial_guess, rhs_force)], axis=0)
    own, place = lax.optimization_barrier((own, place))
    arrived = gather_lateral(own)
    pair = spread_layer(arrived)
    pair_beside = radial(pair)
    viscous, velocity, force, conds, lateral_image, lateral_total, faces = lateral_stage(arrived, pair, *tables)
    radials, total, residual, smoothed, packed = first_stage(
        force, viscous, velocity, lateral_image, lateral_total, *pair_beside
    )
    smoothed_beside = radial(packed)
    coarse = remain_stage(
        conds, radials, total, velocity, residual, smoothed, *smoothed_beside, *tables, faces=faces
    )
    coarse = gather_radial(coarse)
    coefficients = faces_stage(place, *coarse)
    velocity, residual, smoothed, packed = step_stage(
        place, *coarse, *coefficients, *tables, velocity, *pair_beside, smoothed,
        *smoothed_beside, force, conds, radials, total,
    )
    smoothed_beside = radial(packed)
    coarse = remain_stage(conds, radials, total, velocity, residual, smoothed, *smoothed_beside, *tables)
    out = last_stage(place, *gather_radial(coarse), *coefficients, *tables, velocity, smoothed)
    return out.reshape(1, CELLS)


def solution(mesh):
    return jax.shard_map(
        on_device,
        mesh=mesh,
        in_specs=(P("rad", "lat"), P("rad", "lat"), P("rad", "lat"), P(), P(), P()),
        out_specs=P("rad", "lat"),
        check_vma=False,
    )
```

```python
import functools

import jax
import jax.numpy as jnp
from jax import lax
from jax.experimental import pallas as pl
from jax.experimental.pallas import tpu as pltpu
from jax.sharding import PartitionSpec as P

C = 32
HALF = 16
TILES = 64
NR = 16
CHIPS = NR // 2
CELLS = C * C
COARSE = HALF * HALF
LANES = 128
CG_ITERS = 4

cubic_weight = 8.0
radial_weight = 4.0
relax_factor = 0.8


def low(x):
    return lax.broadcasted_iota(jnp.int32, x.shape, x.ndim - 1) < TILES


def swap(x):
    return pltpu.roll(x, TILES, x.ndim - 1)


def pack(a, b):
    return jnp.where(low(a), a, b)


def first_twin(x):
    return jnp.where(low(x), x, swap(x))


def second_twin(x):
    return jnp.where(low(x), swap(x), x)


def glued(values, gluing):
    rows = values.shape[0]
    high = values.astype(jnp.bfloat16)
    rest = values - high.astype(jnp.float32)
    middle = rest.astype(jnp.bfloat16)
    lowest = (rest - middle.astype(jnp.float32)).astype(jnp.bfloat16)
    moved = jnp.dot(
        jnp.concatenate([high, middle, lowest], axis=0), gluing, preferred_element_type=jnp.float32
    )
    return moved[:rows] + (moved[rows : 2 * rows] + moved[2 * rows :])


def fine_ghosts(pad_ref, west_ref, east_ref, gluing, flips):
    north, south = pad_ref[C : 2 * C], pad_ref[CELLS : CELLS + C]
    west, east = pad_ref[pl.ds(C, C, stride=C)], pad_ref[pl.ds(2 * C - 1, C, stride=C)]
    moved = glued(jnp.concatenate([pack(north, south), pack(west, east)], axis=1), gluing)
    mirror = lax.broadcasted_iota(jnp.int32, (C, C), 0) + lax.broadcasted_iota(jnp.int32, (C, C), 1) == C - 1
    mirrored = jnp.dot(
        mirror.astype(jnp.float32), moved, precision=lax.Precision.HIGHEST, preferred_element_type=jnp.float32
    )
    pairs = []
    for pair in range(2):
        lanes = slice(pair * LANES, (pair + 1) * LANES)
        flip = pack(flips[2 * pair : 2 * pair + 1], flips[2 * pair + 1 : 2 * pair + 2])
        pairs.append(jnp.where(flip > 0, mirrored[:, lanes], moved[:, lanes]))
    pad_ref[0:C] = first_twin(pairs[0])
    pad_ref[CELLS + C : CELLS + 2 * C] = second_twin(pairs[0])
    west_ref[...] = first_twin(pairs[1])
    east_ref[...] = second_twin(pairs[1])


def row_of(i):
    return pl.ds(pl.multiple_of(i * C, C), C)


def lateral(pad_ref, west_ref, east_ref, i):
    own = pad_ref[row_of(i + 1)]
    column = lax.broadcasted_iota(jnp.int32, own.shape, 0)
    west = jnp.where(column == 0, west_ref[pl.ds(i, 1)], pltpu.roll(own, 1, 0))
    east = jnp.where(column == C - 1, east_ref[pl.ds(i, 1)], pltpu.roll(own, C - 1, 0))
    return own, (pad_ref[row_of(i)], pad_ref[row_of(i + 2)], west, east)


def coupled(conds, beside):
    total = conds[0] * beside[0]
    for cond, value in zip(conds[1:], beside[1:]):
        total = total + cond * value
    return total


def smooth_row(i, force, cond_total, own, image, residual_ref, smoothed_ref):
    cubic = cubic_weight * own * own
    residual = force - ((cond_total + cubic) * own - image)
    residual_ref[row_of(i)] = residual
    smoothed_ref[row_of(i)] = relax_factor * residual / (cond_total + 3.0 * cubic)


def pack_halves(smoothed_ref, packed_ref):
    packed_ref[...] = pack(smoothed_ref[: CELLS // 2], smoothed_ref[CELLS // 2 :])


def unpack_row(packed_ref, i, upper):
    block = packed_ref[row_of(i)]
    return second_twin(block) if upper else first_twin(block)


def unpack_halves(packed_ref, target_ref):
    target_ref[: CELLS // 2] = first_twin(packed_ref[...])
    target_ref[CELLS // 2 :] = second_twin(packed_ref[...])


def every(ref, start, count):
    return ref[pl.ds(start, count, stride=2)]


def rows_loop(count, step, body):
    @pl.loop(0, count, step=step)
    def _(first):
        for part in range(step):
            body(first + part)


def turned_layer(arrived_ref, first_field, second_field, group):
    parts = [arrived_ref[pl.ds(8 * field + group, TILES, stride=24)] for field in (first_field, second_field)]
    return jnp.concatenate(parts, axis=0).T


def spread_kernel(arrived_ref, pair_ref):
    for group in range(8):
        pair_ref[group * LANES : (group + 1) * LANES] = turned_layer(arrived_ref, 0, 1, group)


def lateral_kernel(
    arrived_ref, pair_ref, gluing_ref, flips_ref, viscous_ref, velocity_ref, force_ref, conds_ref, image_ref,
    total_ref, faces_ref, viscous_pad, viscous_west, viscous_east, pad, west, east,
):
    gluing, flips = gluing_ref[...], flips_ref[...]
    viscous_ref[...] = first_twin(pair_ref[...])
    velocity_ref[...] = second_twin(pair_ref[...])
    viscous_pad[C : C + CELLS] = viscous_ref[...]
    pad[C : C + CELLS] = velocity_ref[...]
    fine_ghosts(viscous_pad, viscous_west, viscous_east, gluing, flips)
    fine_ghosts(pad, west, east, gluing, flips)

    def body(i):
        own, beside = lateral(viscous_pad, viscous_west, viscous_east, i)
        conds = [0.5 * (own + other) for other in beside]
        for direction in range(4):
            conds_ref[direction, row_of(i)] = conds[direction]
        image_ref[row_of(i)] = coupled(conds, lateral(pad, west, east, i)[1])
        total_ref[row_of(i)] = conds[0] + conds[1] + conds[2] + conds[3]

    rows_loop(C, 4, body)
    sums, wests = [], []
    for big in range(HALF):
        upper, lower = big * 2 * C, big * 2 * C + C
        cells = slice(big * HALF, (big + 1) * HALF)

        def both(ref, start):
            return every(ref, start, HALF) + every(ref, start + 1, HALF)

        def column(direction, start):
            ref = conds_ref.at[direction]
            return every(ref, upper + start, HALF) + every(ref, lower + start, HALF)

        faces = pack(both(conds_ref.at[1], lower), column(3, 1))
        faces_ref[cells] = faces
        if big == 0:
            north = both(conds_ref.at[0], upper)
        wests.append(column(2, 0)[0:1])
        sums.append(both(viscous_ref, upper) + both(viscous_ref, lower))
    start = COARSE + COARSE // 2
    edge = pack(north, jnp.concatenate(wests, axis=0))
    for big in range(HALF // 2):
        first = COARSE + big * HALF
        faces_ref[first : first + HALF] = pack(sums[big], sums[big + HALF // 2])
    faces_ref[start : start + HALF] = edge
    for group in range(8):
        force_ref[group * LANES : (group + 1) * LANES] = turned_layer(arrived_ref, 2, 2, group)


def first_kernel(
    force_ref, viscous_ref, velocity_ref, lateral_ref, lateral_total_ref, above_ref, below_ref,
    radials_ref, total_ref, residual_ref, smoothed_ref, packed_ref,
):
    def body(i):
        here = row_of(i)
        viscous, velocity = viscous_ref[here], velocity_ref[here]
        beside = above_ref[here], below_ref[here]
        conds = [radial_weight * 0.5 * (viscous + first_twin(pair)) for pair in beside]
        cond_total = lateral_total_ref[here] + conds[0] + conds[1]
        radials_ref[0, here] = conds[0]
        radials_ref[1, here] = conds[1]
        total_ref[here] = cond_total
        image = lateral_ref[here] + conds[0] * second_twin(beside[0]) + conds[1] * second_twin(beside[1])
        smooth_row(i, force_ref[here], cond_total, velocity, image, residual_ref, smoothed_ref)

    rows_loop(C, 4, body)
    pack_halves(smoothed_ref, packed_ref)


def remain_kernel(
    conds_ref, radials_ref, total_ref, velocity_ref, residual_ref, smoothed_ref, above_ref, below_ref,
    gluing_ref, flips_ref, *rest,
):
    *faces, coarse_ref, pad, west, east, remain, damping = rest
    for faces_ref in faces:
        for copy in range(CHIPS):
            coarse_ref[copy, COARSE:] = faces_ref[...]
    pad[C : C + CELLS] = smoothed_ref[...]
    fine_ghosts(pad, west, east, gluing_ref[...], flips_ref[...])
    for upper in range(2):
        offset = upper * (C // 2)

        def body(source, upper=upper, offset=offset):
            i = source + offset
            here = row_of(i)
            velocity = velocity_ref[here]
            damp = 3.0 * (cubic_weight * velocity * velocity)
            own, beside = lateral(pad, west, east, i)
            beside = beside + (unpack_row(above_ref, source, upper), unpack_row(below_ref, source, upper))
            conds = [conds_ref[direction, here] for direction in range(4)]
            conds += [radials_ref[direction, here] for direction in range(2)]
            image = (total_ref[here] + damp) * own - coupled(conds, beside)
            remain[here] = residual_ref[here] - image
            damping[here] = damp

        rows_loop(C // 2, 4, body)

    for big in range(HALF):
        sums = []
        for ref in (remain, damping):
            start = big * 2 * C
            sums.append(
                every(ref, start, HALF)
                + every(ref, start + 1, HALF)
                + every(ref, start + C, HALF)
                + every(ref, start + C + 1, HALF)
            )
        cells = slice(big * HALF, (big + 1) * HALF)
        sums = pack(sums[0], sums[1])
        for copy in range(CHIPS):
            coarse_ref[copy, cells] = sums


def for_core(place_ref, own_ref, other_ref, body):
    @pl.when(place_ref[0] % 2 == 0)
    def _():
        body(own_ref, other_ref)

    @pl.when(place_ref[0] % 2 == 1)
    def _():
        body(other_ref, own_ref)


def aligned(start, count):
    return pl.ds(pl.multiple_of(start, count), count)


def radial_pair(values):
    swapped = swap(values)
    shaped = swapped.reshape(values.shape[0] // 8, 8, LANES)
    before = pltpu.roll(shaped, 1, 1).reshape(values.shape)
    after = pltpu.roll(shaped, 7, 1).reshape(values.shape)
    return pack(swapped, after), pack(before, swapped)


def faces_kernel(
    place_ref, own_ref, other_ref, rows_ref, columns_ref, up_ref, down_ref, face_total_ref, sums
):
    first, middle, last = COARSE, 2 * COARSE, 2 * COARSE + COARSE // 2
    half = COARSE // 2

    def arrange(even_ref, odd_ref):
        for sub in range(8):
            a, b = even_ref[sub, first:middle], odd_ref[sub, first:middle]
            rows_ref[pl.ds(LANES + sub, COARSE, stride=8)] = pack(a, swap(b))
            east = pack(swap(a), b)
            for big in range(HALF):
                columns_ref[big, pl.ds(8 + sub, HALF, stride=8)] = east[big * HALF : (big + 1) * HALF]
            a, b = even_ref[sub, middle:last], odd_ref[sub, middle:last]
            sums[pl.ds(sub, half, stride=8)] = pack(a, swap(b))
            sums[pl.ds(8 * half + sub, half, stride=8)] = pack(swap(a), b)
            a, b = even_ref[sub, last : last + HALF], odd_ref[sub, last : last + HALF]
            rows_ref[pl.ds(sub, HALF, stride=8)] = pack(a, swap(b))
            west = pack(swap(a), b)
            for big in range(HALF):
                columns_ref[big, sub : sub + 1] = west[big : big + 1]

    for_core(place_ref, own_ref, other_ref, arrange)
    side = HALF * 8
    shape = (side, LANES)
    row = lax.broadcasted_iota(jnp.int32, shape, 0) % 8
    lane = lax.broadcasted_iota(jnp.int32, shape, 1)
    top = (row == 7) & (lane >= TILES)
    bottom = (row == 0) & (lane < TILES)

    @pl.loop(0, HALF)
    def _(big):
        here = pl.ds(pl.multiple_of(big * side, side), side)
        own = sums[here]
        above, below = radial_pair(own)
        up = radial_weight * 0.5 * (own + jnp.where(top, 0.0, above))
        down = radial_weight * 0.5 * (own + jnp.where(bottom, 0.0, below))
        up_ref[here] = jnp.where(top, 0.0, up)
        down_ref[here] = jnp.where(bottom, 0.0, down)
        face_total_ref[here] = (
            rows_ref[here]
            + rows_ref[pl.ds(pl.multiple_of((big + 1) * side, side), side)]
            + columns_ref[big, :side]
            + columns_ref[big, 8 : 8 + side]
            + up
            + down
        )


def coarse_ghosts(pad, gluing, flips):
    side = HALF * 8
    inner = slice(8, 8 + side)
    north, south = pad[1, inner], pad[HALF, inner]
    west = pad[1 : HALF + 1, 8:16].reshape(side, LANES)
    east = pad[1 : HALF + 1, side : side + 8].reshape(side, LANES)
    first = jnp.concatenate([pack(north, swap(south)), pack(west, swap(east))], axis=1)
    second = jnp.concatenate([pack(swap(north), south), pack(swap(west), east)], axis=1)
    moved = glued(jnp.concatenate([first, second], axis=0), gluing)
    ghosts = []
    for pair in range(2):
        lanes = slice(pair * LANES, (pair + 1) * LANES)
        a, b = moved[:side, lanes], moved[side:, lanes]
        ghosts += [pack(a, swap(b)), pack(swap(a), b)]
    for number, ghost in enumerate(ghosts):
        flip = jnp.broadcast_to(flips[number : number + 1], (8, LANES)) > 0
        for k in range(HALF):
            other = HALF - 1 - k
            value = jnp.where(flip, ghost[8 * other : 8 * other + 8], ghost[8 * k : 8 * k + 8])
            if number < 2:
                pad[0 if number == 0 else HALF + 1, 8 + 8 * k : 16 + 8 * k] = value
            else:
                column = 0 if number == 2 else 8 + side
                pad[1 + k, column : column + 8] = value


def total_of(x):
    return jnp.sum(jnp.sum(x, axis=0, keepdims=True), axis=1, keepdims=True)


def folded(x):
    return jnp.sum(x.reshape(x.shape[0] // 8, 8, LANES), axis=0)


def solve_coarse(
    place_ref, own_ref, other_ref, rows_ref, columns_ref, up_ref, down_ref, face_total_ref, gluing, flips,
    pad, diagonal, image, residual, solution,
):
    side = HALF * 8
    inner = slice(8, 8 + side)
    chunk = 64

    def arrange(even_ref, odd_ref):
        for sub in range(8):
            a, b = even_ref[sub, :COARSE], odd_ref[sub, :COARSE]
            residual[pl.ds(sub, COARSE, stride=8)] = pack(a, swap(b))
            diagonal[pl.ds(sub, COARSE, stride=8)] = pack(swap(a), b)

    for_core(place_ref, own_ref, other_ref, arrange)
    zero = jnp.zeros((8, LANES), jnp.float32)

    def here_of(big):
        return pl.ds(pl.multiple_of(big * side, side), side)

    def total_over(body):
        def several(first, total):
            for part in range(4):
                total = body(first * 4 + part, total)
            return total

        return total_of(lax.fori_loop(0, HALF // 4, several, zero))

    def start(big, total):
        here = here_of(big)
        values = residual[here]
        pad[big + 1, inner] = values
        diagonal[here] = diagonal[here] + face_total_ref[here]
        return total + folded(values * values)

    norm = total_over(start)

    def apply_rows(block, total):
        first = block * 4
        for part in range(side // chunk):
            start = part * chunk
            inside = slice(8 + start, 8 + start + chunk)
            before, own = pad[first, inside], pad[first + 1, inside]
            north = rows_ref[aligned(first * side + start, chunk)]
            for big in range(4):
                here = aligned((first + big) * side + start, chunk)
                after = pad[first + big + 2, inside]
                south = rows_ref[aligned((first + big + 1) * side + start, chunk)]
                columns = columns_ref[first + big, start : start + chunk + 8]
                west_end = pad[first + big + 1, start : start + 8]
                east_end = pad[first + big + 1, start + chunk + 8 : start + chunk + 16]
                row = jnp.concatenate([west_end, own, east_end], axis=0)
                above, below = radial_pair(own)
                value = (
                    north * before
                    + south * after
                    + columns[:chunk] * row[:chunk]
                    + columns[8:] * row[16:]
                    + up_ref[here] * above
                    + down_ref[here] * below
                )
                value = diagonal[here] * own - value
                image[here] = value
                total = total + folded(own * value)
                before, own, north = own, after, south
        return total

    for step in range(CG_ITERS):
        coarse_ghosts(pad, gluing, flips)
        length = norm / total_of(lax.fori_loop(0, HALF // 4, apply_rows, zero))

        def advance(big, total, length=length):
            here = here_of(big)
            values = residual[here] - length * image[here]
            residual[here] = values
            return total + folded(values * values)

        ratio = 0.0
        if step + 1 < CG_ITERS:
            following = total_over(advance)
            ratio = following / norm
            norm = following

        def turn(big, total, length=length, ratio=ratio, step=step):
            here = here_of(big)
            old = pad[big + 1, inner]
            solution[here] = length * old if step == 0 else solution[here] + length * old
            if step + 1 < CG_ITERS:
                pad[big + 1, inner] = residual[here] + ratio * old
            return total

        total_over(turn)


def prolong_layer(solution, layer, target):
    inside = (layer >= 0) & (layer < NR)
    place = jnp.clip(layer, 0, NR - 1)
    values = solution[pl.ds(place // 2, COARSE, stride=8)]
    values = jnp.where(place % 2 == 0, first_twin(values), second_twin(values))
    values = jnp.where(inside, values, 0.0)
    for big in range(HALF):
        row = values[big * HALF : (big + 1) * HALF]
        for start in (0, 1, C, C + 1):
            target[pl.ds(big * 2 * C + start, HALF, stride=2)] = row


COARSE_SCRATCH = [
    pltpu.VMEM((HALF + 2, (HALF + 2) * 8, LANES), jnp.float32),
    *[pltpu.VMEM((COARSE * 8, LANES), jnp.float32) for _ in range(4)],
]


def step_kernel(
    place_ref, own_ref, other_ref, rows_ref, columns_ref, up_ref, down_ref, face_total_ref, gluing_ref, flips_ref,
    velocity_ref, above_ref, below_ref, smoothed_ref, smoothed_above_ref, smoothed_below_ref, force_ref,
    conds_ref, radials_ref, total_ref, new_velocity_ref, new_residual_ref, new_smoothed_ref, packed_ref,
    pad, diagonal, image, residual, solution, velocity, west, east, above, below, spread,
):
    gluing, flips = gluing_ref[...], flips_ref[...]
    for pairs, smooth, target in ((above_ref, smoothed_above_ref, above), (below_ref, smoothed_below_ref, below)):
        unpack_halves(smooth, target)
        target[...] = target[...] + second_twin(pairs[...])
    solve_coarse(
        place_ref, own_ref, other_ref, rows_ref, columns_ref, up_ref, down_ref, face_total_ref, gluing, flips,
        pad, diagonal, image, residual, solution,
    )
    layer = place_ref[0]
    prolong_layer(solution, layer, spread)
    velocity[C : C + CELLS] = velocity_ref[...] + smoothed_ref[...] + spread[...]
    new_velocity_ref[...] = velocity[C : C + CELLS]
    fine_ghosts(velocity, west, east, gluing, flips)
    for shift, target in ((1, above), (-1, below)):
        prolong_layer(solution, layer + shift, spread)
        target[...] = target[...] + spread[...]

    def body(i):
        here = row_of(i)
        own, beside = lateral(velocity, west, east, i)
        beside = beside + (above[here], below[here])
        conds = [conds_ref[direction, here] for direction in range(4)]
        conds += [radials_ref[direction, here] for direction in range(2)]
        smooth_row(i, force_ref[here], total_ref[here], own, coupled(conds, beside), new_residual_ref, new_smoothed_ref)

    rows_loop(C, 4, body)
    pack_halves(new_smoothed_ref, packed_ref)


def last_kernel(
    place_ref, own_ref, other_ref, rows_ref, columns_ref, up_ref, down_ref, face_total_ref, gluing_ref, flips_ref,
    velocity_ref, smoothed_ref, out_ref, pad, diagonal, image, residual, solution, spread, turned,
):
    solve_coarse(
        place_ref, own_ref, other_ref, rows_ref, columns_ref, up_ref, down_ref, face_total_ref,
        gluing_ref[...], flips_ref[...], pad, diagonal, image, residual, solution,
    )
    prolong_layer(solution, place_ref[0], spread)
    for group in range(8):
        cells = slice(group * LANES, (group + 1) * LANES)
        turned[cells] = (velocity_ref[cells] + smoothed_ref[cells] + spread[cells]).T
    for group in range(8):
        out_ref[group : group + 1] = turned[pl.ds(group * LANES + place_ref[1], 1)]


def call(kernel, outs, scratch, args, scalars=0, mebibytes=4):
    vmem = pl.BlockSpec(memory_space=pltpu.VMEM)
    shapes = [jax.ShapeDtypeStruct(shape, jnp.float32) for shape in outs]
    return pl.pallas_call(
        kernel,
        out_shape=shapes,
        in_specs=[pl.BlockSpec(memory_space=pltpu.SMEM)] * scalars + [vmem] * (len(args) - scalars),
        out_specs=[vmem] * len(outs),
        scratch_shapes=[pltpu.VMEM(shape, jnp.float32) for shape in scratch],
        compiler_params=pltpu.CompilerParams(vmem_limit_bytes=VMEM_MIB << 20),
        cost_estimate=pl.CostEstimate(flops=mebibytes << 20, bytes_accessed=mebibytes << 20, transcendentals=0),
    )(*args)


VMEM_MIB = 20
PADDED = (CELLS + 2 * C, LANES)
FINE = (CELLS, LANES)
PACKED = (CELLS // 2, LANES)
EDGE = (C, LANES)
FACES = (COARSE + COARSE // 2 + HALF, LANES)
GRID = (COARSE * 8, LANES)
COARSE_SCRATCH = [(HALF + 2, (HALF + 2) * 8, LANES)] + [GRID] * 4


def spread_layer(arrived):
    return call(spread_kernel, [FINE], [], [arrived])[0]


def lateral_stage(*args):
    outs = [FINE, FINE, FINE, (4,) + FINE, FINE, FINE, FACES]
    return call(lateral_kernel, outs, [PADDED, EDGE, EDGE, PADDED, EDGE, EDGE], args, mebibytes=24)


def first_stage(*args):
    return call(first_kernel, [(2,) + FINE, FINE, FINE, FINE, PACKED], [], args)


def remain_stage(*args, faces=None):
    rows = COARSE
    if faces is not None:
        args, rows = args + (faces,), COARSE + FACES[0]
    return call(remain_kernel, [(CHIPS, rows, LANES)], [PADDED, EDGE, EDGE, FINE, FINE], args)[0]


def faces_stage(*args):
    outs = [((HALF + 1) * HALF * 8, LANES), (HALF, (HALF + 1) * 8, LANES)] + [GRID] * 3
    return call(faces_kernel, outs, [GRID], args, 1, 24)


def step_stage(*args):
    scratch = COARSE_SCRATCH + [PADDED, EDGE, EDGE, FINE, FINE, FINE]
    return call(step_kernel, [FINE, FINE, FINE, PACKED], scratch, args, 1)


def last_stage(*args):
    return call(last_kernel, [(8, LANES)], COARSE_SCRATCH + [FINE, FINE], args, 1)[0]


NEAR = 8
FAR = TILES // NEAR


def place_of(tile):
    return tile % NEAR * FAR + tile // NEAR


def gluing_tables(glue_tile, glue_side, glue_flip):
    def lanes_of(table):
        return table.reshape(FAR, NEAR, 4).transpose(2, 1, 0).reshape(4, TILES)

    source = (lanes_of(glue_side) * TILES + place_of(lanes_of(glue_tile))).reshape(1, 4 * TILES)
    gluing = (jnp.arange(4 * TILES)[:, None] == source).astype(jnp.bfloat16)
    flips = lanes_of(glue_flip).astype(jnp.float32)
    flips = jnp.concatenate([flips, flips], axis=1)
    return gluing, jnp.concatenate([flips, flips], axis=0)


def gather(values, axis, groups):
    sent = jnp.broadcast_to(values[None], (len(groups[0]),) + values.shape)
    arrived = lax.all_to_all(sent, axis, split_axis=0, concat_axis=0, axis_index_groups=groups, tiled=True)
    return arrived.reshape((-1,) + values.shape[1:])


def gather_lateral(values):
    tiles = sorted(range(TILES), key=place_of)
    far = [tiles[near * FAR : (near + 1) * FAR] for near in range(NEAR)]
    return gather(gather(values, "lat", far), "lat", [list(group) for group in zip(*far)])


def gather_cores(copies):
    groups = []
    for tile in range(TILES):
        for core in range(2):
            group = []
            for chip in range(CHIPS):
                other = tile ^ 1 if chip % 4 == 3 else tile
                group.append(other * NR + 2 * chip + core)
            groups.append(group)
    return lax.all_to_all(
        copies, ("lat", "rad"), split_axis=0, concat_axis=0, axis_index_groups=groups, tiled=True
    )


def swap_cores(own):
    return lax.ppermute(own, "rad", [(layer, layer ^ 1) for layer in range(NR)])


def gather_radial(copies):
    own = gather_cores(copies)
    return own, swap_cores(own)


def radial(values):
    lat = lax.axis_size("lat")
    above, below = [], []
    for tile in range(lat):
        for layer in range(NR - 1):
            other = tile ^ 1 if layer % 4 == 3 else tile
            above.append((other * NR + layer + 1, tile * NR + layer))
            below.append((tile * NR + layer, other * NR + layer + 1))
    return lax.ppermute(values, ("lat", "rad"), above), lax.ppermute(values, ("lat", "rad"), below)


def on_device(rhs_force, viscosity, initial_guess, glue_tile, glue_side, glue_flip):
    tables = gluing_tables(glue_tile, glue_side, glue_flip)
    place = jnp.stack([lax.axis_index("rad"), place_of(lax.axis_index("lat"))]).astype(jnp.int32)
    own = jnp.concatenate([field.reshape(8, LANES) for field in (viscosity, initial_guess, rhs_force)], axis=0)
    own, place = lax.optimization_barrier((own, place))
    arrived = gather_lateral(own)
    pair = spread_layer(arrived)
    pair_beside = radial(pair)
    viscous, velocity, force, conds, lateral_image, lateral_total, faces = lateral_stage(arrived, pair, *tables)
    radials, total, residual, smoothed, packed = first_stage(
        force, viscous, velocity, lateral_image, lateral_total, *pair_beside
    )
    smoothed_beside = radial(packed)
    coarse = remain_stage(
        conds, radials, total, velocity, residual, smoothed, *smoothed_beside, *tables, faces=faces
    )
    coarse = gather_radial(coarse)
    coefficients = faces_stage(place, *coarse)
    velocity, residual, smoothed, packed = step_stage(
        place, *coarse, *coefficients, *tables, velocity, *pair_beside, smoothed,
        *smoothed_beside, force, conds, radials, total,
    )
    smoothed_beside = radial(packed)
    coarse = remain_stage(conds, radials, total, velocity, residual, smoothed, *smoothed_beside, *tables)
    out = last_stage(place, *gather_radial(coarse), *coefficients, *tables, velocity, smoothed)
    return out.reshape(1, CELLS)


def solution(mesh):
    return jax.shard_map(
        on_device,
        mesh=mesh,
        in_specs=(P("rad", "lat"), P("rad", "lat"), P("rad", "lat"), P(), P(), P()),
        out_specs=P("rad", "lat"),
        check_vma=False,
    )
```
